32 devices in a mesh: ctx: 8 (over y, x, core), tp: 4 (over z).
Axes of the slice: x: 2, y: 2, z: 4, core: 2. Of those that a mesh axis runs over, the one named last changes fastest.
Arguments:
- value_path: bfloat16 [1024, 8192], P('ctx', 'tp'), may hold values from -6 to 6
- key_se: bfloat16 [1024, 8192], P('ctx', 'tp'), may hold values from -6 to 6
- query_se: bfloat16 [1024, 8192], P('ctx', 'tp'), may hold values from -60 to 60
- key_mr: bfloat16 [1024, 8192], P('ctx', 'tp'), may hold values from -6 to 6
- query_mr: bfloat16 [1024, 8192], P('ctx', 'tp'), may hold values from -6 to 6
- out_grad: bfloat16 [1024, 8192], P('ctx', 'tp'), may hold values from -6 to 6
- norm_gain: bfloat16 [8192], P('tp'), may hold values from 0.099609375 to 1.8984375
- filter_se: bfloat16 [7, 8192], P(None, 'tp'), may hold values from -2 to 2
- filter_mr: bfloat16 [128, 8192], P(None, 'tp'), may hold values from -0.5 to 0.5
Outputs:
- grad_value: bfloat16 [1024, 8192], P('ctx', 'tp')
- grad_query_se: bfloat16 [1024, 8192], P('ctx', 'tp')
- grad_key_se: bfloat16 [1024, 8192], P('ctx', 'tp')
- grad_query_mr: bfloat16 [1024, 8192], P('ctx', 'tp')
- grad_key_mr: bfloat16 [1024, 8192], P('ctx', 'tp')
- grad_filter_se: float32 [7, 8192], P(None, 'tp')
- grad_filter_mr: float32 [128, 8192], P(None, 'tp')
- grad_gain: float32 [8192], P('tp')
The draws below stay inside these ranges and needn't reach their ends.
All inputs are finite; a program needn't handle non-finite values.
Results may differ from the reference program's by a relative error of at most 0.015.
Values may be sent and summed in bfloat16 or wider, within the bound.
A program may use at most 64 MiB of HBM per device.

```python
import math
import jax
import jax.numpy as jnp
from jax import lax

D = 8192
SE_TAPS = 7
MR_TAPS = 128
TOKENS = 1024


def draw_query_se(key, part):
    key = jax.random.fold_in(key, 11)
    key_base, key_cols, key_rows = jax.random.split(key, 3)
    base = jnp.clip(jax.random.normal(key_base, (TOKENS, D), jnp.float32), -6.0, 6.0)
    position = jnp.arange(D, dtype=jnp.float32) / D
    cols = jnp.exp(math.log(10.0) * (0.5 * position + 0.5 * jax.random.uniform(key_cols, (D,), jnp.float32)))
    rows = jnp.exp(math.log(10.0) * jax.random.uniform(key_rows, (TOKENS, 1), jnp.float32))
    return (base * cols[None, :] * rows / 10.0).astype(jnp.bfloat16)


def shard_levels(key, shape, pieces, smallest, high):
    factor_of = 1.0
    for dim, shards_of in pieces:
        steps = jax.random.uniform(jax.random.fold_in(jax.random.fold_in(key, 6), dim), (shards_of,), jnp.float32, smallest / len(pieces), high / len(pieces))
        factor_of = factor_of * jnp.repeat(jnp.exp(steps), shape[dim] // shards_of).reshape((-1,) + (1,) * (len(shape) - 1 - dim))
    return factor_of


def noise(rng, extent, deviation, reach, cuts=(), held_as=jnp.bfloat16):
    values = jax.random.normal(rng, extent, jnp.float32) * deviation
    if len(cuts) > 0:
        values = shard_levels(rng, extent, cuts, -0.22, 0.18) * values
    return jnp.clip(values, min=-reach, max=reach).astype(held_as)


def setup_inputs(seed: int = 0) -> dict:
    keys = jax.random.split(jax.random.key(seed), 10)
    value_path = noise(keys[0], (TOKENS, D), 1.0, 6.0, ((0, 8), (1, 4)))
    key_se = noise(keys[1], (TOKENS, D), 1.0, 6.0, ((0, 8), (1, 4)))
    query_se = draw_query_se(jax.random.fold_in(keys[9], 71), 0)
    key_mr = noise(keys[3], (TOKENS, D), 1.0, 6.0, ((0, 8), (1, 4)))
    query_mr = noise(keys[4], (TOKENS, D), 1.0, 6.0, ((0, 8), (1, 4)))
    out_grad = noise(keys[5], (TOKENS, D), 1.0, 6.0, ((0, 8), (1, 4)))
    norm_gain = jnp.clip(1.0 + 0.18 * jax.random.normal(keys[6], (D,), jnp.float32), 0.099609375, 1.8984375).astype(jnp.bfloat16)
    filter_se = noise(keys[7], (SE_TAPS, D), SE_TAPS ** -0.5, 2.0, ((1, 4),))
    filter_mr = noise(keys[8], (MR_TAPS, D), MR_TAPS ** -0.5, 0.5, ((1, 4),))
    return {"value_path": value_path, "key_se": key_se, "query_se": query_se, "key_mr": key_mr, "query_mr": query_mr, "out_grad": out_grad, "norm_gain": norm_gain, "filter_se": filter_se, "filter_mr": filter_mr}


def causal_conv(padded, kernel, length):
    taps = kernel.shape[0]
    kern = kernel.astype(jnp.float32)

    def add_tap(index, total):
        tap = jnp.asarray(index).astype(jnp.int32)
        start = (jnp.int32(taps - 1) - tap).astype(jnp.int32)
        piece = lax.dynamic_slice_in_dim(padded, start, length, 0).astype(jnp.float32)
        weight_row = lax.dynamic_slice_in_dim(kern, tap, 1, 0)
        return total + piece * weight_row
    empty = jnp.zeros((length, padded.shape[1]), jnp.float32)
    return lax.fori_loop(0, taps, add_tap, empty)

def anti_conv(padded, kernel, length):
    taps = kernel.shape[0]
    kern = kernel.astype(jnp.float32)

    def add_tap(index, total):
        tap = jnp.asarray(index).astype(jnp.int32)
        piece = lax.dynamic_slice_in_dim(padded, tap, length, 0).astype(jnp.float32)
        weight_row = lax.dynamic_slice_in_dim(kern, tap, 1, 0)
        return total + piece * weight_row
    empty = jnp.zeros((length, padded.shape[1]), jnp.float32)
    return lax.fori_loop(0, taps, add_tap, empty)

def filter_grad(padded, grad_conv, taps, length):
    grad_f = grad_conv.astype(jnp.float32)

    def one_tap(carry, index):
        tap = index.astype(jnp.int32)
        start = (jnp.int32(taps - 1) - tap).astype(jnp.int32)
        piece = lax.dynamic_slice_in_dim(padded, start, length, 0).astype(jnp.float32)
        return (carry, lax.optimization_barrier(jnp.sum(grad_f * piece, axis=0)))
    tap_index = jnp.arange(taps).astype(jnp.int32)
    carry, rows = lax.scan(one_tap, jnp.zeros((), jnp.float32), tap_index)
    return rows

def reference(value_path, key_se, query_se, key_mr, query_mr, out_grad, norm_gain, filter_se, filter_mr):
    f32 = jnp.float32
    bf16 = jnp.bfloat16
    length = value_path.shape[0]
    prod_se = (key_se.astype(f32) * value_path.astype(f32)).astype(bf16)
    pad_se = jnp.pad(prod_se, ((SE_TAPS - 1, 0), (0, 0)))
    conv_se = causal_conv(pad_se, filter_se, length)
    mixed_se = query_se.astype(f32) * conv_se
    inv_rms = lax.rsqrt(lax.optimization_barrier(jnp.sum(mixed_se * mixed_se, axis=1, keepdims=True)) / D + 1e-06)
    gain = norm_gain.astype(f32)
    normed = (mixed_se * inv_rms * gain).astype(bf16)
    prod_mr = (key_mr.astype(f32) * normed.astype(f32)).astype(bf16)
    pad_mr = jnp.pad(prod_mr, ((MR_TAPS - 1, 0), (0, 0)))
    conv_mr = causal_conv(pad_mr, filter_mr, length)
    grad_query_mr = (out_grad.astype(f32) * conv_mr).astype(bf16)
    grad_conv_mr = (out_grad.astype(f32) * query_mr.astype(f32)).astype(bf16)
    grad_prod_mr = anti_conv(jnp.pad(grad_conv_mr, ((0, MR_TAPS - 1), (0, 0))), filter_mr, length)
    grad_key_mr = (grad_prod_mr * normed.astype(f32)).astype(bf16)
    grad_filter_mr = filter_grad(pad_mr, grad_conv_mr, MR_TAPS, length)
    grad_normed = grad_prod_mr * key_mr.astype(f32)
    scaled = grad_normed * gain
    grad_gain = lax.optimization_barrier(jnp.sum(grad_normed * mixed_se * inv_rms, axis=0))
    dot_sum = lax.optimization_barrier(jnp.sum(scaled * mixed_se, axis=1, keepdims=True))
    grad_mixed = inv_rms * scaled - mixed_se * (inv_rms * inv_rms * inv_rms) * dot_sum / D
    grad_query_se = (grad_mixed * conv_se).astype(bf16)
    grad_conv_se = (grad_mixed * query_se.astype(f32)).astype(bf16)
    grad_prod_se = anti_conv(jnp.pad(grad_conv_se, ((0, SE_TAPS - 1), (0, 0))), filter_se, length)
    grad_key_se = (grad_prod_se * value_path.astype(f32)).astype(bf16)
    grad_value = (grad_prod_se * key_se.astype(f32)).astype(bf16)
    grad_filter_se = filter_grad(pad_se, grad_conv_se, SE_TAPS, length)
    return (grad_value, grad_query_se, grad_key_se, grad_query_mr, grad_key_mr, grad_filter_se, grad_filter_mr, grad_gain)
```

```python
import functools
import math

import jax
import jax.numpy as jnp
import ml_dtypes
import numpy as np
from jax import lax
from jax.experimental import pallas as pl
from jax.experimental.pallas import tpu as pltpu
from jax.sharding import PartitionSpec as P

D = 8192
CW = 256
PIECES = 4
F32 = jnp.float32
BF16 = jnp.bfloat16


def split(m):
    hi = m.astype(ml_dtypes.bfloat16)
    lo = (m - hi.astype(np.float64)).astype(ml_dtypes.bfloat16)
    return hi, lo


def matrices(rows):
    n = 2 * rows
    theta = 2.0 * math.pi * (np.arange(rows) + 0.5) / n
    ang = theta[:, None] * np.arange(n)[None, :]
    fwd = np.concatenate([np.cos(ang), -np.sin(ang)], axis=0)
    bwd = np.concatenate([np.cos(ang).T, -np.sin(ang).T], axis=1) / rows
    fh, fl = split(fwd)
    near = np.concatenate([fh[:, :rows], fl[:, :rows]], axis=1)
    far = np.concatenate([fh[:, rows:], fl[:, rows:]], axis=1)
    bh, bl = split(bwd)
    return np.stack([fh, fl, near, far, bh, bl])


def body(
    n, ntp, fused, eps,
    vp, ks, qs, km, qm, og, gain, fse, fmr, mats,
    o_val, o_qse, o_kse, o_qmr, o_kmr, o_small, o_fmr,
    win_se, g2, wsend, wh, conv, fs, os_, gp, win_gs, acc, row_send, row_recv, inv_send, invl_row, inv2, invl2, k2,
    pfb, own, rc, sx, rx, ag_own, ag_x, ag_c, sm, rs_s, ag_s,
    tail_sem, gh_s, gh_r, wh_s, wh_r, row_s, row_r, inv_sem, gs_sem,
    rc_s, rc_r, rx_s, rx_r, agx_s, agx_r, agc_s, agc_r, rss_s, rss_r, ags_s, ags_r,
):
    me = lax.axis_index("ctx")
    tp = lax.axis_index("tp")
    rows, chans = vp.shape
    taps = fse.shape[0]
    nc = chans // CW
    hc = chans // PIECES
    per = hc // CW
    has_l = me > 0
    has_r = me < n - 1
    left = (me + n - 1) % n
    right = (me + 1) % n
    mesh_ids = pl.DeviceIdType.MESH

    def remote(src, dst, ssem, rsem, where):
        return pltpu.make_async_remote_copy(
            src_ref=src, dst_ref=dst, send_sem=ssem, recv_sem=rsem, device_id=where, device_id_type=mesh_ids
        )

    def lanes(c):
        return pl.ds(pl.multiple_of(c * CW, CW), CW)

    def wide(ref):
        return jnp.concatenate([ref[...]] * (CW // 128), axis=1)

    bar = pltpu.get_barrier_semaphore()
    ctx_peers = [(me + d) % n for d in range(1, n)] if fused else [left, right]
    for p in ctx_peers:
        pl.semaphore_signal(bar, inc=1, device_id={"ctx": p}, device_id_type=mesh_ids)
    for d in range(1, ntp):
        pl.semaphore_signal(bar, inc=1, device_id={"tp": (tp + d) % ntp}, device_id_type=mesh_ids)

    @pl.when(jnp.logical_not(has_l))
    def _():
        win_se[pl.ds(0, 8), :] = jnp.zeros((8, chans), F32)
        wh[...] = jnp.zeros_like(wh)
        invl_row[...] = jnp.zeros_like(invl_row)

    @pl.when(jnp.logical_not(has_r))
    def _():
        g2[pl.ds(rows, rows), :] = jnp.zeros((rows, chans), BF16)
        win_gs[pl.ds(rows, 8), :] = jnp.zeros((8, chans), F32)

    @pl.loop(0, nc)
    def _(c):
        ch = lanes(c)
        win_se[pl.ds(8, rows), ch] = (ks[:, ch].astype(F32) * vp[:, ch].astype(F32)).astype(BF16).astype(F32)
        g2[pl.ds(0, rows), ch] = (og[:, ch].astype(F32) * qm[:, ch].astype(F32)).astype(BF16)

    pl.semaphore_wait(bar, len(ctx_peers) + ntp - 1)

    tail = remote(win_se.at[pl.ds(rows, 8)], win_se.at[pl.ds(0, 8)], tail_sem.at[0], tail_sem.at[1], {"ctx": right})

    def g_piece(h):
        hl = pl.ds(pl.multiple_of(h * hc, hc), hc)
        return remote(g2.at[pl.ds(0, rows), hl], g2.at[pl.ds(rows, rows), hl], gh_s.at[h], gh_r.at[h], {"ctx": left})

    def w_piece(h):
        hl = pl.ds(pl.multiple_of(h * hc, hc), hc)
        return remote(wsend.at[:, hl], wh.at[:, hl], wh_s.at[h], wh_r.at[h], {"ctx": right})

    @pl.when(has_r)
    def _():
        tail.start()

    @pl.when(has_l)
    def _():
        for h in range(PIECES):
            g_piece(h).start()
        tail.wait_recv()

    acc[...] = jnp.zeros_like(acc)

    def fold(x):
        s = x[:, :128]
        for i in range(1, CW // 128):
            s = s + x[:, i * 128 : (i + 1) * 128]
        return s

    @pl.loop(0, PIECES)
    def _(h):
        for i in range(per):
            ch = lanes(h * per + i)
            f = fse[:, ch].astype(F32)
            cs = win_se[pl.ds(8, rows), ch] * f[0:1]
            for j in range(1, taps):
                cs = cs + win_se[pl.ds(8 - j, rows), ch] * f[j : j + 1]
            conv[:, ch] = cs
            mixed = qs[:, ch].astype(F32) * cs
            acc[...] += fold(mixed * mixed)
            wsend[:, ch] = (mixed * gain[:, ch] * km[:, ch].astype(F32)).astype(BF16)

        @pl.when(has_r)
        def _():
            w_piece(h).start()

    def share(k):
        row_send[k] = jnp.broadcast_to(jnp.sum(acc[...].T, axis=0, keepdims=True), (8, 128))
        for d in range(1, ntp):
            row_copy(k, d).start()

    def row_copy(k, d):
        return remote(
            row_send.at[k], row_recv.at[k, d - 1], row_s.at[k, d - 1], row_r.at[k, d - 1], {"tp": (tp + d) % ntp}
        )

    def gather(k):
        for d in range(1, ntp):
            row_copy(k, d).wait()
        total = row_send[k]
        for d in range(1, ntp):
            total = total + row_recv[k, d - 1]
        return total

    share(0)

    def twice(x):
        return jnp.concatenate([x, x], axis=0)

    def dot(a, b):
        return jnp.dot(a, b, preferred_element_type=F32)

    def back(y, at):
        hi = y.astype(BF16)
        lo = (y - hi.astype(F32)).astype(BF16)
        bh = mats[4, pl.ds(at, rows), :]
        bl = mats[5, pl.ds(at, rows), :]
        return dot(bh, hi) + (dot(bl, hi) + dot(bh, lo))

    @pl.loop(0, nc)
    def _(c):
        ch = lanes(c)
        fs[:, ch] = dot(mats[2], twice(fmr[:, ch]))
        os_[:, ch] = dot(mats[2], twice(g2[pl.ds(0, rows), ch]))

    inv_row = lax.rsqrt(gather(0) / D + 1e-06)
    inv_send[...] = inv_row
    inv_copy = remote(inv_send, invl_row, inv_sem.at[0], inv_sem.at[1], {"ctx": right})

    @pl.when(has_r)
    def _():
        inv_copy.start()

    inv2[...] = jnp.broadcast_to(inv_row[0:1], (128, 128)).T

    acc[...] = jnp.zeros_like(acc)

    @pl.loop(0, PIECES)
    def _(h):
        @pl.when(has_l)
        def _():
            g_piece(h).wait_send()

        @pl.when(has_r)
        def _():
            g_piece(h).wait_recv()

        for i in range(per):
            ch = lanes(h * per + i)
            g = os_[:, ch] + dot(mats[3], twice(g2[pl.ds(rows, rows), ch]))
            gr, gi = g[:rows], g[rows:]
            fr, fi = fs[pl.ds(0, rows), ch], fs[pl.ds(rows, rows), ch]
            grad = back(jnp.concatenate([gr * fr + gi * fi, gi * fr - gr * fi], axis=0), 0)
            gp[:, ch] = grad
            mixed = qs[:, ch].astype(F32) * conv[:, ch]
            normed = (mixed * wide(inv2) * gain[:, ch]).astype(BF16)
            o_kmr[:, ch] = (grad * normed.astype(F32)).astype(BF16)
            acc[...] += fold(grad * km[:, ch].astype(F32) * gain[:, ch] * mixed)

    share(1)

    @pl.when(has_l)
    def _():
        inv_copy.wait_recv()
        for h in range(PIECES):
            w_piece(h).wait_recv()

    invl2[...] = jnp.broadcast_to(invl_row[0:1], (128, 128)).T

    def medium(c):
        ch = lanes(c)
        kmf = km[:, ch].astype(F32)
        mixed = qs[:, ch].astype(F32) * conv[:, ch]
        normed = (mixed * wide(inv2) * gain[:, ch]).astype(BF16)
        prod = (kmf * normed.astype(F32)).astype(BF16)
        halo = (wh[:, ch].astype(F32) * wide(invl2)).astype(BF16)
        window = jnp.concatenate([halo, prod], axis=0)
        x = dot(mats[0], window) + dot(mats[1], window)
        xr, xi = x[:rows], x[rows:]
        gr, gi = os_[pl.ds(0, rows), ch], os_[pl.ds(rows, rows), ch]
        fr, fi = fs[pl.ds(0, rows), ch], fs[pl.ds(rows, rows), ch]
        part = -back(jnp.concatenate([gr * xr + gi * xi, gi * xr - gr * xi], axis=0), rows)
        y = back(jnp.concatenate([xr * fr - xi * fi, xr * fi + xi * fr], axis=0), rows)
        o_qmr[:, ch] = (og[:, ch].astype(F32) * y).astype(BF16)
        return part

    if fused:
        chips = n // 2
        core = me % 2
        chip = me // 2
        mate = me + 1 - 2 * core

        def to_mate(i):
            return remote(pfb.at[i], rc.at[i], rc_s.at[i], rc_r.at[i], {"ctx": mate})

        def to_chip(d):
            return remote(
                sx.at[d - 1], rx.at[d - 1], rx_s.at[d - 1], rx_r.at[d - 1], {"ctx": ((chip + d) % chips) * 2 + core}
            )

        def all_chip(d):
            return remote(
                ag_own, ag_x.at[d - 1], agx_s.at[d - 1], agx_r.at[d - 1], {"ctx": ((chip + d) % chips) * 2 + core}
            )

        def all_mate(d):
            src = ag_own if d == 0 else ag_x.at[d - 1]
            return remote(src, ag_c.at[d], agc_s.at[d], agc_r.at[d], {"ctx": mate})

        @pl.loop(0, chips)
        def _(i):
            pfb[i] = medium(2 * i + 1 - core).astype(BF16)
            to_mate(i).start()

        @pl.loop(0, chips)
        def _(i):
            own[i] = medium(2 * i + core)

        for d in range(1, chips):
            to = (chip + d) % chips
            to_mate(to).wait_recv()
            sx[d - 1] = (own[to] + rc[to].astype(F32)).astype(BF16)
            to_chip(d).start()
    else:

        @pl.loop(0, nc)
        def _(c):
            o_fmr[:, lanes(c)] = medium(c).astype(o_fmr.dtype)

    dot_row = gather(1)
    inv = inv2[...]
    k2[...] = inv * inv * inv * jnp.broadcast_to(dot_row[0:1], (128, 128)).T / D

    @pl.loop(0, nc)
    def _(c):
        ch = lanes(c)
        cs = conv[:, ch]
        q = qs[:, ch].astype(F32)
        mixed = q * cs
        inv_w = wide(inv2)
        grad_normed = gp[:, ch] * km[:, ch].astype(F32)
        grad_mixed = inv_w * (grad_normed * gain[:, ch]) - mixed * wide(k2)
        o_qse[:, ch] = (grad_mixed * cs).astype(BF16)
        gcs = (grad_mixed * q).astype(BF16).astype(F32)
        win_gs[pl.ds(0, rows), ch] = gcs
        for j in range(taps):
            sm[c, pl.ds(j, 1), :] = jnp.sum(gcs * win_se[pl.ds(8 - j, rows), ch], axis=0, keepdims=True)
        sm[c, pl.ds(taps, 1), :] = jnp.sum(grad_normed * mixed * inv_w, axis=0, keepdims=True)

    head = remote(win_gs.at[pl.ds(0, 8)], win_gs.at[pl.ds(rows, 8)], gs_sem.at[0], gs_sem.at[1], {"ctx": left})

    @pl.when(has_l)
    def _():
        head.start()

    if fused:

        def small_to(d):
            return remote(
                sm.at[(me + d) % n], rs_s.at[d - 1], rss_s.at[d - 1], rss_r.at[d - 1], {"ctx": (me + d) % n}
            )

        def small_all(d):
            return remote(
                ag_s.at[0], ag_s.at[d], ags_s.at[d - 1], ags_r.at[d - 1], {"ctx": (me + d) % n}
            )

        for d in range(1, n):
            small_to(d).start()

        to_mate(chip).wait_recv()
        total = own[chip] + rc[chip].astype(F32)
        for d in range(1, chips):
            to_chip(d).wait_recv()
            total = total + rx[d - 1].astype(F32)
        ag_own[...] = total.astype(BF16)
        for d in range(1, chips):
            all_chip(d).start()
        all_mate(0).start()

        total_s = sm[me]
        for d in range(1, n):
            small_to(d).wait_recv()
            total_s = total_s + rs_s[d - 1]
        ag_s[0] = total_s
        for d in range(1, n):
            small_all(d).start()

    @pl.when(has_r)
    def _():
        head.wait_recv()

    @pl.loop(0, nc)
    def _(c):
        ch = lanes(c)
        f = fse[:, ch].astype(F32)
        g = win_gs[pl.ds(0, rows), ch] * f[0:1]
        for j in range(1, taps):
            g = g + win_gs[pl.ds(j, rows), ch] * f[j : j + 1]
        o_kse[:, ch] = (g * vp[:, ch].astype(F32)).astype(BF16)
        o_val[:, ch] = (g * ks[:, ch].astype(F32)).astype(BF16)

    if fused:
        for d in range(1, chips):
            all_chip(d).wait_recv()
            all_mate(d).start()
        o_fmr[:, lanes(me)] = ag_own[...]
        for d in range(1, chips):
            o_fmr[:, lanes(((chip + chips - d) % chips) * 2 + core)] = ag_x[d - 1]
        o_small[:, lanes(me)] = ag_s[0]
        for d in range(1, n):
            small_all(d).wait_recv()
            o_small[:, lanes((me + n - d) % n)] = ag_s[d]
        for d in range(chips):
            all_mate(d).wait_recv()
            o_fmr[:, lanes(((chip + chips - d) % chips) * 2 + 1 - core)] = ag_c[d]
        for i in range(chips):
            to_mate(i).wait_send()
            all_mate(i).wait_send()
        for d in range(1, chips):
            to_chip(d).wait_send()
            all_chip(d).wait_send()
        for d in range(1, n):
            small_to(d).wait_send()
            small_all(d).wait_send()
    else:

        @pl.loop(0, nc)
        def _(c):
            o_small[:, lanes(c)] = sm[c]

    @pl.when(has_l)
    def _():
        head.wait_send()

    @pl.when(has_r)
    def _():
        tail.wait_send()
        inv_copy.wait_send()
        for h in range(PIECES):
            w_piece(h).wait_send()


def shards(n, ntp, vp, ks, qs, km, qm, og, norm_gain, fse, fmr):
    rows, chans = vp.shape
    taps = fse.shape[0]
    nc = chans // CW
    fused = n == nc and n % 2 == 0
    chips = max(n // 2, 2) if fused else 2
    blk = (rows, CW)
    peers = n if fused else 2
    wide_out = jax.ShapeDtypeStruct((rows, chans), BF16)
    dma = pltpu.SemaphoreType.DMA
    vmem = pltpu.VMEM
    scratch = [
        vmem((rows + 8, chans), F32),
        vmem((2 * rows, chans), BF16),
        vmem((rows, chans), BF16),
        vmem((rows, chans), BF16),
        vmem((rows, chans), F32),
        vmem((2 * rows, chans), F32),
        vmem((2 * rows, chans), F32),
        vmem((rows, chans), F32),
        vmem((rows + 8, chans), F32),
        vmem((rows, 128), F32),
        vmem((2, 8, 128), F32),
        vmem((2, ntp - 1, 8, 128), F32),
        vmem((8, 128), F32),
        vmem((8, 128), F32),
        vmem((rows, 128), F32),
        vmem((rows, 128), F32),
        vmem((rows, 128), F32),
        vmem((chips,) + blk, BF16),
        vmem((chips,) + blk, F32),
        vmem((chips,) + blk, BF16),
        vmem((chips - 1,) + blk, BF16),
        vmem((chips - 1,) + blk, BF16),
        vmem(blk, BF16),
        vmem((chips - 1,) + blk, BF16),
        vmem((chips,) + blk, BF16),
        vmem((nc, taps + 1, CW), F32),
        vmem((peers - 1, taps + 1, CW), F32),
        vmem((peers, taps + 1, CW), F32),
        dma((2,)),
        dma((PIECES,)), dma((PIECES,)),
        dma((PIECES,)), dma((PIECES,)),
        dma((2, ntp - 1)), dma((2, ntp - 1)),
        dma((2,)),
        dma((2,)),
        dma((chips,)), dma((chips,)),
        dma((chips - 1,)), dma((chips - 1,)),
        dma((chips - 1,)), dma((chips - 1,)),
        dma((chips,)), dma((chips,)),
        dma((peers - 1,)), dma((peers - 1,)),
        dma((peers - 1,)), dma((peers - 1,)),
    ]
    spec = pl.BlockSpec(memory_space=pltpu.VMEM)
    mats = jnp.asarray(matrices(rows))
    outs = pl.pallas_call(
        functools.partial(body, n, ntp, fused, 1e-06),
        out_shape=[wide_out] * 5
        + [jax.ShapeDtypeStruct((taps + 1, chans), F32), jax.ShapeDtypeStruct((rows, chans), BF16 if fused else F32)],
        in_specs=[spec] * 10,
        out_specs=[spec] * 7,
        scratch_shapes=scratch,
        compiler_params=pltpu.CompilerParams(
            collective_id=0, has_side_effects=True, vmem_limit_bytes=48 * 1024 * 1024
        ),
        name="hyena_backward",
    )(vp, ks, qs, km, qm, og, norm_gain.astype(F32).reshape(1, chans), fse, fmr, mats)
    o_val, o_qse, o_kse, o_qmr, o_kmr, small, gf = outs
    if not fused:
        small, gf = lax.psum((small, gf), "ctx")
    return o_val, o_qse, o_kse, o_qmr, o_kmr, small[:taps], gf.astype(F32), small[taps]


def solution(mesh):
    tok = P("ctx", "tp")
    fil = P(None, "tp")
    return jax.shard_map(
        functools.partial(shards, mesh.shape["ctx"], mesh.shape["tp"]),
        mesh=mesh,
        in_specs=(tok,) * 6 + (P("tp"), fil, fil),
        out_specs=(tok,) * 5 + (fil, fil, P("tp")),
        check_vma=False,
    )
```

```python
import functools
import math

import jax
import jax.numpy as jnp
import ml_dtypes
import numpy as np
from jax import lax
from jax.experimental import pallas as pl
from jax.experimental.pallas import tpu as pltpu
from jax.sharding import PartitionSpec as P

D = 8192
CW = 256
PIECES = 4
F32 = jnp.float32
BF16 = jnp.bfloat16


def split(m):
    hi = m.astype(ml_dtypes.bfloat16)
    lo = (m - hi.astype(np.float64)).astype(ml_dtypes.bfloat16)
    return hi, lo


def matrices(rows):
    n = 2 * rows
    theta = 2.0 * math.pi * (np.arange(rows) + 0.5) / n
    ang = theta[:, None] * np.arange(n)[None, :]
    fwd = np.concatenate([np.cos(ang), -np.sin(ang)], axis=0)
    bwd = np.concatenate([np.cos(ang).T, -np.sin(ang).T], axis=1) / rows
    fh, fl = split(fwd)
    near = np.concatenate([fh[:, :rows], fl[:, :rows]], axis=1)
    far = np.concatenate([fh[:, rows:], fl[:, rows:]], axis=1)
    bh, bl = split(bwd)
    first = np.concatenate([bh[:rows], bl[:rows]], axis=0)
    last = np.concatenate([bh[rows:], bl[rows:]], axis=0)
    return np.stack([fh, fl, near, far, first, last])


def body(
    n, ntp, fused,
    vp_h, ks_h, qs_h, km_h, qm_h, og_h, gain_h, fse_h, fmr_h, mats_h,
    o_val, o_qse, o_kse, o_qmr, o_kmr, o_small, o_fmr,
    vp, ks, qs, km, qm, og, gain_in, gain, fse, fmr, mats, in_sem,
    win_se, g2, wsend, wh, conv, fs, os_, gp, win_gs, acc, row_send, row_recv, inv_send, invl_row, inv2, invl2, k2,
    pfb, own, rc, sx, rx, ag_own, ag_x, ag_c, sm, rs_s, ag_s,
    tail_sem, gh_s, gh_r, wh_s, wh_r, row_s, row_r, inv_sem, gs_sem,
    rc_s, rc_r, rx_s, rx_r, agx_s, agx_r, agc_s, agc_r, rss_s, rss_r, ags_s, ags_r,
):
    me = lax.axis_index("ctx")
    tp = lax.axis_index("tp")
    rows, chans = vp.shape
    taps = fse.shape[0]
    nc = chans // CW
    hc = chans // PIECES
    per = hc // CW
    has_l = me > 0
    has_r = me < n - 1
    left = (me + n - 1) % n
    right = (me + 1) % n
    mesh_ids = pl.DeviceIdType.MESH

    def remote(src, dst, ssem, rsem, where):
        return pltpu.make_async_remote_copy(
            src_ref=src, dst_ref=dst, send_sem=ssem, recv_sem=rsem, device_id=where, device_id_type=mesh_ids
        )

    def lanes(c):
        return pl.ds(pl.multiple_of(c * CW, CW), CW)

    def wide(ref):
        return jnp.concatenate([ref[...]] * (CW // 128), axis=1)

    fetch = [
        pltpu.make_async_copy(src, dst, in_sem.at[i])
        for i, (src, dst) in enumerate(
            [(og_h, og), (qm_h, qm), (ks_h, ks), (vp_h, vp), (qs_h, qs), (fse_h, fse), (gain_h, gain_in), (km_h, km),
             (mats_h, mats), (fmr_h, fmr)]
        )
    ]
    for copy in fetch:
        copy.start()

    bar = pltpu.get_barrier_semaphore()
    ctx_peers = [(me + d) % n for d in range(1, n)] if fused else [left, right]
    for p in ctx_peers:
        pl.semaphore_signal(bar, inc=1, device_id={"ctx": p}, device_id_type=mesh_ids)
    for d in range(1, ntp):
        pl.semaphore_signal(bar, inc=1, device_id={"tp": (tp + d) % ntp}, device_id_type=mesh_ids)

    @pl.when(jnp.logical_not(has_l))
    def _():
        win_se[pl.ds(0, 8), :] = jnp.zeros((8, chans), F32)
        wh[...] = jnp.zeros_like(wh)
        invl_row[...] = jnp.zeros_like(invl_row)

    @pl.when(jnp.logical_not(has_r))
    def _():
        g2[pl.ds(rows, rows), :] = jnp.zeros((rows, chans), BF16)
        win_gs[pl.ds(rows, 8), :] = jnp.zeros((8, chans), F32)

    for copy in fetch[:4]:
        copy.wait()

    @pl.loop(0, nc)
    def _(c):
        ch = lanes(c)
        win_se[pl.ds(8, rows), ch] = (ks[:, ch].astype(F32) * vp[:, ch].astype(F32)).astype(BF16).astype(F32)
        g2[pl.ds(0, rows), ch] = (og[:, ch].astype(F32) * qm[:, ch].astype(F32)).astype(BF16)

    pl.semaphore_wait(bar, len(ctx_peers) + ntp - 1)

    tail = remote(win_se.at[pl.ds(rows, 8)], win_se.at[pl.ds(0, 8)], tail_sem.at[0], tail_sem.at[1], {"ctx": right})

    def g_piece(h):
        hl = pl.ds(pl.multiple_of(h * hc, hc), hc)
        return remote(g2.at[pl.ds(0, rows), hl], g2.at[pl.ds(rows, rows), hl], gh_s.at[h], gh_r.at[h], {"ctx": left})

    def w_piece(h):
        hl = pl.ds(pl.multiple_of(h * hc, hc), hc)
        return remote(wsend.at[:, hl], wh.at[:, hl], wh_s.at[h], wh_r.at[h], {"ctx": right})

    @pl.when(has_r)
    def _():
        tail.start()

    @pl.when(has_l)
    def _():
        for h in range(PIECES):
            g_piece(h).start()
        tail.wait_recv()

    for copy in fetch[4:8]:
        copy.wait()
    gain[...] = gain_in[...].astype(F32).reshape(1, chans)
    acc[...] = jnp.zeros_like(acc)

    def fold(x):
        s = x[:, :128]
        for i in range(1, CW // 128):
            s = s + x[:, i * 128 : (i + 1) * 128]
        return s

    @pl.loop(0, PIECES)
    def _(step):
        h = (right // 2 + 1 + step) % PIECES
        for i in range(per):
            ch = lanes(h * per + i)
            f = fse[:, ch].astype(F32)
            cs = win_se[pl.ds(8, rows), ch] * f[0:1]
            for j in range(1, taps):
                cs = cs + win_se[pl.ds(8 - j, rows), ch] * f[j : j + 1]
            conv[:, ch] = cs
            mixed = qs[:, ch].astype(F32) * cs
            acc[...] += fold(mixed * mixed)
            wsend[:, ch] = (mixed * gain[:, ch] * km[:, ch].astype(F32)).astype(BF16)

        @pl.when(has_r)
        def _():
            w_piece(h).start()

    def share(k):
        row_send[k] = jnp.broadcast_to(jnp.sum(acc[...].T, axis=0, keepdims=True), (8, 128))
        for d in range(1, ntp):
            row_copy(k, d).start()

    def row_copy(k, d):
        return remote(
            row_send.at[k], row_recv.at[k, d - 1], row_s.at[k, d - 1], row_r.at[k, d - 1], {"tp": (tp + d) % ntp}
        )

    def gather(k):
        for d in range(1, ntp):
            row_copy(k, d).wait()
        total = row_send[k]
        for d in range(1, ntp):
            total = total + row_recv[k, d - 1]
        return total

    share(0)

    def twice(x):
        return jnp.concatenate([x, x], axis=0)

    def dot(a, b):
        return jnp.dot(a, b, preferred_element_type=F32)

    def back(re, im, which):
        both = dot(mats[which], jnp.concatenate([re.astype(BF16), im.astype(BF16)], axis=0))
        return both[:rows] + both[rows:]

    for copy in fetch[8:]:
        copy.wait()

    @pl.loop(0, nc)
    def _(c):
        ch = lanes(c)
        fs[:, ch] = dot(mats[2], twice(fmr[:, ch]))
        os_[:, ch] = dot(mats[2], twice(g2[pl.ds(0, rows), ch]))

    inv_row = lax.rsqrt(gather(0) / D + 1e-06)
    inv_send[...] = inv_row
    inv_copy = remote(inv_send, invl_row, inv_sem.at[0], inv_sem.at[1], {"ctx": right})

    @pl.when(has_r)
    def _():
        inv_copy.start()

    inv2[...] = jnp.broadcast_to(inv_row[0:1], (128, 128)).T

    acc[...] = jnp.zeros_like(acc)

    @pl.loop(0, PIECES)
    def _(h):
        @pl.when(has_l)
        def _():
            g_piece(h).wait_send()

        @pl.when(has_r)
        def _():
            g_piece(h).wait_recv()

        for i in range(per):
            ch = lanes(h * per + i)
            g = os_[:, ch] + dot(mats[3], twice(g2[pl.ds(rows, rows), ch]))
            gr, gi = g[:rows], g[rows:]
            fr, fi = fs[pl.ds(0, rows), ch], fs[pl.ds(rows, rows), ch]
            grad = back(gr * fr + gi * fi, gi * fr - gr * fi, 4)
            gp[:, ch] = grad
            mixed = qs[:, ch].astype(F32) * conv[:, ch]
            normed = (mixed * wide(inv2) * gain[:, ch]).astype(BF16)
            o_kmr[:, ch] = (grad * normed.astype(F32)).astype(BF16)
            acc[...] += fold(grad * km[:, ch].astype(F32) * gain[:, ch] * mixed)

    share(1)

    @pl.when(has_l)
    def _():
        inv_copy.wait_recv()

    invl2[...] = jnp.broadcast_to(invl_row[0:1], (128, 128)).T

    def medium(c):
        ch = lanes(c)
        kmf = km[:, ch].astype(F32)
        mixed = qs[:, ch].astype(F32) * conv[:, ch]
        normed = (mixed * wide(inv2) * gain[:, ch]).astype(BF16)
        prod = (kmf * normed.astype(F32)).astype(BF16)
        halo = (wh[:, ch].astype(F32) * wide(invl2)).astype(BF16)
        window = jnp.concatenate([halo, prod], axis=0)
        x = dot(mats[0], window) + dot(mats[1], window)
        xr, xi = x[:rows], x[rows:]
        gr, gi = os_[pl.ds(0, rows), ch], os_[pl.ds(rows, rows), ch]
        fr, fi = fs[pl.ds(0, rows), ch], fs[pl.ds(rows, rows), ch]
        part = -back(gr * xr + gi * xi, gi * xr - gr * xi, 5)
        y = back(xr * fr - xi * fi, xr * fi + xi * fr, 5)
        o_qmr[:, ch] = (og[:, ch].astype(F32) * y).astype(BF16)
        return part

    if fused:
        chips = n // 2
        core = me % 2
        chip = me // 2
        mate = me + 1 - 2 * core

        def to_mate(i):
            return remote(pfb.at[i], rc.at[i], rc_s.at[i], rc_r.at[i], {"ctx": mate})

        def to_chip(d):
            return remote(
                sx.at[d - 1], rx.at[d - 1], rx_s.at[d - 1], rx_r.at[d - 1], {"ctx": ((chip + d) % chips) * 2 + core}
            )

        def all_chip(d):
            return remote(
                ag_own, ag_x.at[d - 1], agx_s.at[d - 1], agx_r.at[d - 1], {"ctx": ((chip + d) % chips) * 2 + core}
            )

        def all_mate(d):
            src = ag_own if d == 0 else ag_x.at[d - 1]
            return remote(src, ag_c.at[d], agc_s.at[d], agc_r.at[d], {"ctx": mate})

        @pl.loop(1, chips + 1)
        def _(d):
            c = (chip + d) % chips

            @pl.when(has_l)
            def _():
                w_piece(c).wait_recv()

            pfb[c] = medium(2 * c + 1 - core).astype(BF16)
            to_mate(c).start()
            part = medium(2 * c + core)
            to_mate(c).wait_recv()
            own[...] = part + rc[c].astype(F32)

            @pl.when(d < chips)
            def _():
                sx[d - 1] = own[...].astype(BF16)
                to_chip(d).start()
    else:

        @pl.when(has_l)
        def _():
            for h in range(PIECES):
                w_piece(h).wait_recv()

        @pl.loop(0, nc)
        def _(c):
            o_fmr[:, lanes(c)] = medium(c).astype(o_fmr.dtype)

    dot_row = gather(1)
    inv = inv2[...]
    k2[...] = inv * inv * inv * jnp.broadcast_to(dot_row[0:1], (128, 128)).T / D

    @pl.loop(0, nc)
    def _(c):
        ch = lanes(c)
        cs = conv[:, ch]
        q = qs[:, ch].astype(F32)
        mixed = q * cs
        inv_w = wide(inv2)
        grad_normed = gp[:, ch] * km[:, ch].astype(F32)
        grad_mixed = inv_w * (grad_normed * gain[:, ch]) - mixed * wide(k2)
        o_qse[:, ch] = (grad_mixed * cs).astype(BF16)
        gcs = (grad_mixed * q).astype(BF16).astype(F32)
        win_gs[pl.ds(0, rows), ch] = gcs
        for j in range(taps):
            sm[c, pl.ds(j, 1), :] = jnp.sum(gcs * win_se[pl.ds(8 - j, rows), ch], axis=0, keepdims=True)
        sm[c, pl.ds(taps, 1), :] = jnp.sum(grad_normed * mixed * inv_w, axis=0, keepdims=True)

    head = remote(win_gs.at[pl.ds(0, 8)], win_gs.at[pl.ds(rows, 8)], gs_sem.at[0], gs_sem.at[1], {"ctx": left})

    @pl.when(has_l)
    def _():
        head.start()

    if fused:

        def small_to(d):
            return remote(
                sm.at[(me + d) % n], rs_s.at[d - 1], rss_s.at[d - 1], rss_r.at[d - 1], {"ctx": (me + d) % n}
            )

        def small_all(d):
            return remote(
                ag_s.at[0], ag_s.at[d], ags_s.at[d - 1], ags_r.at[d - 1], {"ctx": (me + d) % n}
            )

        for d in range(1, n):
            small_to(d).start()

        total = own[...]
        for d in range(1, chips):
            to_chip(d).wait_recv()
            total = total + rx[d - 1].astype(F32)
        ag_own[...] = total.astype(BF16)
        for d in range(1, chips):
            all_chip(d).start()
        all_mate(0).start()

        total_s = sm[me]
        for d in range(1, n):
            small_to(d).wait_recv()
            total_s = total_s + rs_s[d - 1]
        ag_s[0] = total_s
        for d in range(1, n):
            small_all(d).start()

    @pl.when(has_r)
    def _():
        head.wait_recv()

    @pl.loop(0, nc)
    def _(c):
        ch = lanes(c)
        f = fse[:, ch].astype(F32)
        g = win_gs[pl.ds(0, rows), ch] * f[0:1]
        for j in range(1, taps):
            g = g + win_gs[pl.ds(j, rows), ch] * f[j : j + 1]
        o_kse[:, ch] = (g * vp[:, ch].astype(F32)).astype(BF16)
        o_val[:, ch] = (g * ks[:, ch].astype(F32)).astype(BF16)

    if fused:
        for d in range(1, chips):
            all_chip(d).wait_recv()
            all_mate(d).start()
        o_fmr[:, lanes(me)] = ag_own[...]
        for d in range(1, chips):
            o_fmr[:, lanes(((chip + chips - d) % chips) * 2 + core)] = ag_x[d - 1]
        o_small[:, lanes(me)] = ag_s[0]
        for d in range(1, n):
            small_all(d).wait_recv()
            o_small[:, lanes((me + n - d) % n)] = ag_s[d]
        for d in range(chips):
            all_mate(d).wait_recv()
            o_fmr[:, lanes(((chip + chips - d) % chips) * 2 + 1 - core)] = ag_c[d]
        for i in range(chips):
            to_mate(i).wait_send()
            all_mate(i).wait_send()
        for d in range(1, chips):
            to_chip(d).wait_send()
            all_chip(d).wait_send()
        for d in range(1, n):
            small_to(d).wait_send()
            small_all(d).wait_send()
    else:

        @pl.loop(0, nc)
        def _(c):
            o_small[:, lanes(c)] = sm[c]

    @pl.when(has_l)
    def _():
        head.wait_send()

    @pl.when(has_r)
    def _():
        tail.wait_send()
        inv_copy.wait_send()
        for h in range(PIECES):
            w_piece(h).wait_send()


def write_out(val, qse, kse, qmr, kmr, small, gf, *rest):
    outs, (o_fse, o_fmr, o_gain, fse, fmr, gain, sem) = rest[:5], rest[5:]
    copies = [pltpu.make_async_copy(a, b, sem.at[i]) for i, (a, b) in enumerate(zip((val, qse, kse, qmr, kmr), outs))]
    for copy in copies:
        copy.start()
    taps = fse.shape[0]
    part = fmr.shape[0] // 4
    for i in range(4):
        at = pl.ds(i * part, part)
        fmr[at, :] = gf[at, :].astype(F32)
        copies.append(pltpu.make_async_copy(fmr.at[at], o_fmr.at[at], sem.at[5 + i]))
        copies[-1].start()
    fse[...] = small[pl.ds(0, taps), :]
    gain[...] = small[pl.ds(taps, 1), :]
    copies.append(pltpu.make_async_copy(fse, o_fse, sem.at[9]))
    copies.append(pltpu.make_async_copy(gain, o_gain, sem.at[10]))
    copies[-2].start()
    copies[-1].start()
    for copy in copies:
        copy.wait()


def shards(n, ntp, vp, ks, qs, km, qm, og, norm_gain, fse, fmr):
    rows, chans = vp.shape
    taps = fse.shape[0]
    nc = chans // CW
    fused = n == nc and n % 2 == 0
    chips = max(n // 2, 2) if fused else 2
    blk = (rows, CW)
    peers = n if fused else 2
    wide_out = jax.ShapeDtypeStruct((rows, chans), BF16)
    dma = pltpu.SemaphoreType.DMA
    vmem = pltpu.VMEM
    scratch = [vmem((rows, chans), BF16) for _ in range(6)] + [
        vmem((chans,), BF16),
        vmem((1, chans), F32),
        vmem((taps, chans), BF16),
        vmem(fmr.shape, BF16),
        vmem((6, 2 * rows, 2 * rows), BF16),
        dma((10,)),
        vmem((rows + 8, chans), F32),
        vmem((2 * rows, chans), BF16),
        vmem((rows, chans), BF16),
        vmem((rows, chans), BF16),
        vmem((rows, chans), F32),
        vmem((2 * rows, chans), F32),
        vmem((2 * rows, chans), F32),
        vmem((rows, chans), F32),
        vmem((rows + 8, chans), F32),
        vmem((rows, 128), F32),
        vmem((2, 8, 128), F32),
        vmem((2, ntp - 1, 8, 128), F32),
        vmem((8, 128), F32),
        vmem((8, 128), F32),
        vmem((rows, 128), F32),
        vmem((rows, 128), F32),
        vmem((rows, 128), F32),
        vmem((chips,) + blk, BF16),
        vmem(blk, F32),
        vmem((chips,) + blk, BF16),
        vmem((chips - 1,) + blk, BF16),
        vmem((chips - 1,) + blk, BF16),
        vmem(blk, BF16),
        vmem((chips - 1,) + blk, BF16),
        vmem((chips,) + blk, BF16),
        vmem((nc, taps + 1, CW), F32),
        vmem((peers - 1, taps + 1, CW), F32),
        vmem((peers, taps + 1, CW), F32),
        dma((2,)),
        dma((PIECES,)), dma((PIECES,)),
        dma((PIECES,)), dma((PIECES,)),
        dma((2, ntp - 1)), dma((2, ntp - 1)),
        dma((2,)),
        dma((2,)),
        dma((chips,)), dma((chips,)),
        dma((chips - 1,)), dma((chips - 1,)),
        dma((chips - 1,)), dma((chips - 1,)),
        dma((chips,)), dma((chips,)),
        dma((peers - 1,)), dma((peers - 1,)),
        dma((peers - 1,)), dma((peers - 1,)),
    ]
    spec = pl.BlockSpec(memory_space=pltpu.VMEM)
    mats = jnp.asarray(matrices(rows))
    operands = (vp, ks, qs, km, qm, og, norm_gain, fse, fmr, mats)
    outs = pl.pallas_call(
        functools.partial(body, n, ntp, fused),
        out_shape=[wide_out] * 5
        + [jax.ShapeDtypeStruct((taps + 1, chans), F32), jax.ShapeDtypeStruct((rows, chans), BF16 if fused else F32)],
        in_specs=[pl.BlockSpec(memory_space=pltpu.HBM)] * 10,
        out_specs=[spec] * 7,
        scratch_shapes=scratch,
        compiler_params=pltpu.CompilerParams(
            collective_id=0, has_side_effects=True, vmem_limit_bytes=40 * 1024 * 1024
        ),
        name="hyena_backward",
    )(*(pltpu.with_memory_space_constraint(x, pltpu.HBM) for x in operands))
    if not fused:
        small, gf = lax.psum(outs[5:], "ctx")
        outs = list(outs[:5]) + [small, gf]
    hbm = pl.BlockSpec(memory_space=pltpu.HBM)
    done = pl.pallas_call(
        write_out,
        out_shape=[wide_out] * 5
        + [
            jax.ShapeDtypeStruct((taps, chans), F32),
            jax.ShapeDtypeStruct((rows, chans), F32),
            jax.ShapeDtypeStruct((1, chans), F32),
        ],
        in_specs=[spec] * 7,
        out_specs=[hbm] * 8,
        scratch_shapes=[vmem((taps, chans), F32), vmem((rows, chans), F32), vmem((1, chans), F32), dma((11,))],
        compiler_params=pltpu.CompilerParams(vmem_limit_bytes=12 * 1024 * 1024),
        name="write_out",
    )(*outs)
    return tuple(done[:7]) + (done[7].reshape(chans),)


def solution(mesh):
    tok = P("ctx", "tp")
    fil = P(None, "tp")
    return jax.shard_map(
        functools.partial(shards, mesh.shape["ctx"], mesh.shape["tp"]),
        mesh=mesh,
        in_specs=(tok,) * 6 + (P("tp"), fil, fil),
        out_specs=(tok,) * 5 + (fil, fil, P("tp")),
        check_vma=False,
    )
```

```python
import functools
import math

import jax
import jax.numpy as jnp
import ml_dtypes
import numpy as np
from jax import lax
from jax.experimental import pallas as pl
from jax.experimental.pallas import tpu as pltpu
from jax.sharding import PartitionSpec as P

D = 8192
CW = 256
PIECES = 4
F32 = jnp.float32
BF16 = jnp.bfloat16


def split(m):
    hi = m.astype(ml_dtypes.bfloat16)
    lo = (m - hi.astype(np.float64)).astype(ml_dtypes.bfloat16)
    return hi, lo


def matrices(rows):
    n = 2 * rows
    theta = 2.0 * math.pi * (np.arange(rows) + 0.5) / n
    ang = theta[:, None] * np.arange(n)[None, :]
    fwd = np.concatenate([np.cos(ang), -np.sin(ang)], axis=0)
    bwd = np.concatenate([np.cos(ang).T, -np.sin(ang).T], axis=1) / rows
    fh, fl = split(fwd)
    near = np.concatenate([fh[:, :rows], fl[:, :rows]], axis=1)
    far = np.concatenate([fh[:, rows:], fl[:, rows:]], axis=1)
    bh, bl = split(bwd)
    first = np.concatenate([bh[:rows], bl[:rows]], axis=0)
    last = np.concatenate([bh[rows:], bl[rows:]], axis=0)
    return np.stack([fh, fl, near, far, first, last])


def body(
    n, ntp, fused,
    vp_h, ks_h, qs_h, km_h, qm_h, og_h, gain_h, fse_h, fmr_h, mats_h,
    o_val, o_qse, o_kse, o_qmr, o_kmr, o_small, o_fmr,
    vp, ks, qs, km, qm, og, gain_in, gain, fse, fmr, mats, in_sem,
    win_se, g2, wsend, wh, conv, fs, os_, xs, gp, win_gs, acc, row_send, row_recv, inv_send, invl_row, inv2, invl2, k2,
    pfb, own, rc, sx, rx, ag_own, ag_x, ag_c, sm, rs_s, ag_s,
    tail_sem, gh_s, gh_r, wh_s, wh_r, row_s, row_r, inv_sem, gs_sem,
    rc_s, rc_r, rx_s, rx_r, agx_s, agx_r, agc_s, agc_r, rss_s, rss_r, ags_s, ags_r,
):
    me = lax.axis_index("ctx")
    tp = lax.axis_index("tp")
    rows, chans = vp.shape
    taps = fse.shape[0]
    nc = chans // CW
    hc = chans // PIECES
    per = hc // CW
    tiles = CW // 128
    has_l = me > 0
    has_r = me < n - 1
    left = (me + n - 1) % n
    right = (me + 1) % n
    mesh_ids = pl.DeviceIdType.MESH

    def remote(src, dst, ssem, rsem, where):
        return pltpu.make_async_remote_copy(
            src_ref=src, dst_ref=dst, send_sem=ssem, recv_sem=rsem, device_id=where, device_id_type=mesh_ids
        )

    def lanes(c):
        return pl.ds(pl.multiple_of(c * CW, CW), CW)

    def tile(t):
        return pl.ds(pl.multiple_of(t * 128, 128), 128)

    def wide(ref):
        return jnp.concatenate([ref[...]] * (CW // 128), axis=1)

    fetch = [
        pltpu.make_async_copy(src, dst, in_sem.at[i])
        for i, (src, dst) in enumerate(
            [(og_h, og), (qm_h, qm), (ks_h, ks), (vp_h, vp), (qs_h, qs), (fse_h, fse), (gain_h, gain_in), (km_h, km),
             (mats_h, mats), (fmr_h, fmr)]
        )
    ]
    for copy in fetch:
        copy.start()

    bar = pltpu.get_barrier_semaphore()
    ctx_peers = [(me + d) % n for d in range(1, n)] if fused else [left, right]
    for p in ctx_peers:
        pl.semaphore_signal(bar, inc=1, device_id={"ctx": p}, device_id_type=mesh_ids)
    for d in range(1, ntp):
        pl.semaphore_signal(bar, inc=1, device_id={"tp": (tp + d) % ntp}, device_id_type=mesh_ids)

    @pl.when(jnp.logical_not(has_l))
    def _():
        win_se[:, pl.ds(0, 8), :] = jnp.zeros((chans // 128, 8, 128), F32)
        wh[...] = jnp.zeros_like(wh)
        invl_row[...] = jnp.zeros_like(invl_row)

    @pl.when(jnp.logical_not(has_r))
    def _():
        g2[pl.ds(rows, rows), :] = jnp.zeros((rows, chans), BF16)
        win_gs[:, pl.ds(rows, 8), :] = jnp.zeros((chans // 128, 8, 128), F32)

    for copy in fetch[:4]:
        copy.wait()

    @pl.loop(0, nc)
    def _(c):
        ch = lanes(c)
        g2[pl.ds(0, rows), ch] = (og[:, ch].astype(F32) * qm[:, ch].astype(F32)).astype(BF16)
        prod = (ks[:, ch].astype(F32) * vp[:, ch].astype(F32)).astype(BF16).astype(F32)
        for i in range(tiles):
            win_se[c * tiles + i, pl.ds(8, rows), :] = prod[:, i * 128 : (i + 1) * 128]

    pl.semaphore_wait(bar, len(ctx_peers) + ntp - 1)

    tail = remote(win_se.at[:, pl.ds(rows, 8)], win_se.at[:, pl.ds(0, 8)], tail_sem.at[0], tail_sem.at[1], {"ctx": right})

    def g_piece(h):
        hl = pl.ds(pl.multiple_of(h * hc, hc), hc)
        return remote(g2.at[pl.ds(0, rows), hl], g2.at[pl.ds(rows, rows), hl], gh_s.at[h], gh_r.at[h], {"ctx": left})

    def w_piece(h):
        hl = pl.ds(pl.multiple_of(h * hc, hc), hc)
        return remote(wsend.at[:, hl], wh.at[:, hl], wh_s.at[h], wh_r.at[h], {"ctx": right})

    @pl.when(has_r)
    def _():
        tail.start()

    @pl.when(has_l)
    def _():
        for h in range(PIECES):
            g_piece(h).start()
        tail.wait_recv()

    for copy in fetch[4:8]:
        copy.wait()
    gain[...] = gain_in[...].astype(F32).reshape(1, chans)
    acc[...] = jnp.zeros_like(acc)

    def fold(x):
        s = x[:, :128]
        for i in range(1, CW // 128):
            s = s + x[:, i * 128 : (i + 1) * 128]
        return s

    @pl.loop(0, PIECES)
    def _(step):
        h = (right // 2 + 1 + step) % PIECES
        for i in range(hc // 128):
            t = h * (hc // 128) + i
            ch = tile(t)
            f = fse[:, ch].astype(F32)
            cs = win_se[t, pl.ds(8, rows), :] * f[0:1]
            for j in range(1, taps):
                cs = cs + win_se[t, pl.ds(8 - j, rows), :] * f[j : j + 1]
            conv[:, ch] = cs
            mixed = qs[:, ch].astype(F32) * cs
            acc[...] += mixed * mixed
            wsend[:, ch] = (mixed * gain[:, ch] * km[:, ch].astype(F32)).astype(BF16)

        @pl.when(has_r)
        def _():
            w_piece(h).start()

    def share(k):
        row_send[k] = jnp.broadcast_to(jnp.sum(acc[...].T, axis=0, keepdims=True), (8, 128))
        for d in range(1, ntp):
            row_copy(k, d).start()

    def row_copy(k, d):
        return remote(
            row_send.at[k], row_recv.at[k, d - 1], row_s.at[k, d - 1], row_r.at[k, d - 1], {"tp": (tp + d) % ntp}
        )

    def gather(k):
        for d in range(1, ntp):
            row_copy(k, d).wait()
        total = row_send[k]
        for d in range(1, ntp):
            total = total + row_recv[k, d - 1]
        return total

    share(0)

    def twice(x):
        return jnp.concatenate([x, x], axis=0)

    def dot(a, b):
        return jnp.dot(a, b, preferred_element_type=F32)

    def back(re, im, which):
        both = dot(mats[which], jnp.concatenate([re.astype(BF16), im.astype(BF16)], axis=0))
        return both[:rows] + both[rows:]

    for copy in fetch[8:]:
        copy.wait()

    @pl.loop(0, PIECES)
    def _(h):
        for i in range(per):
            ch = lanes(h * per + i)
            fs[:, ch] = dot(mats[2], twice(fmr[:, ch]))
            os_[:, ch] = dot(mats[2], twice(g2[pl.ds(0, rows), ch]))

    inv_row = lax.rsqrt(gather(0) / D + 1e-06)
    inv_send[...] = inv_row
    inv_copy = remote(inv_send, invl_row, inv_sem.at[0], inv_sem.at[1], {"ctx": right})

    @pl.when(has_r)
    def _():
        inv_copy.start()

    inv2[...] = jnp.broadcast_to(inv_row[0:1], (128, 128)).T

    acc[...] = jnp.zeros_like(acc)

    @pl.loop(0, PIECES)
    def _(h):
        @pl.when(has_l)
        def _():
            g_piece(h).wait_send()

        @pl.when(has_r)
        def _():
            g_piece(h).wait_recv()

        for i in range(per):
            ch = lanes(h * per + i)
            g = os_[:, ch] + dot(mats[3], twice(g2[pl.ds(rows, rows), ch]))
            gr, gi = g[:rows], g[rows:]
            fr, fi = fs[pl.ds(0, rows), ch], fs[pl.ds(rows, rows), ch]
            grad = back(gr * fr + gi * fi, gi * fr - gr * fi, 4)
            gp[:, ch] = grad
            mixed = qs[:, ch].astype(F32) * conv[:, ch]
            normed = (mixed * wide(inv2) * gain[:, ch]).astype(BF16)
            o_kmr[:, ch] = (grad * normed.astype(F32)).astype(BF16)
            acc[...] += fold(grad * km[:, ch].astype(F32) * gain[:, ch] * mixed)

    share(1)

    @pl.when(has_l)
    def _():
        inv_copy.wait_recv()

    invl2[...] = jnp.broadcast_to(invl_row[0:1], (128, 128)).T

    def medium(c):
        ch = lanes(c)
        kmf = km[:, ch].astype(F32)
        mixed = qs[:, ch].astype(F32) * conv[:, ch]
        normed = (mixed * wide(inv2) * gain[:, ch]).astype(BF16)
        prod = (kmf * normed.astype(F32)).astype(BF16)
        halo = (wh[:, ch].astype(F32) * wide(invl2)).astype(BF16)
        window = jnp.concatenate([halo, prod], axis=0)
        x = dot(mats[0], window) + dot(mats[1], window)
        xr, xi = x[:rows], x[rows:]
        xs[:, ch] = x
        gr, gi = os_[pl.ds(0, rows), ch], os_[pl.ds(rows, rows), ch]
        return -back(gr * xr + gi * xi, gi * xr - gr * xi, 5)

    def medium_out(c):
        ch = lanes(c)
        xr, xi = xs[pl.ds(0, rows), ch], xs[pl.ds(rows, rows), ch]
        fr, fi = fs[pl.ds(0, rows), ch], fs[pl.ds(rows, rows), ch]
        y = back(xr * fr - xi * fi, xr * fi + xi * fr, 5)
        o_qmr[:, ch] = (og[:, ch].astype(F32) * y).astype(BF16)

    if fused:
        chips = n // 2
        core = me % 2
        chip = me // 2
        mate = me + 1 - 2 * core

        def to_mate(i):
            return remote(pfb.at[i], rc.at[i], rc_s.at[i], rc_r.at[i], {"ctx": mate})

        def to_chip(d):
            return remote(
                sx.at[d - 1], rx.at[d - 1], rx_s.at[d - 1], rx_r.at[d - 1], {"ctx": ((chip + d) % chips) * 2 + core}
            )

        def all_chip(d):
            return remote(
                ag_own, ag_x.at[d - 1], agx_s.at[d - 1], agx_r.at[d - 1], {"ctx": ((chip + d) % chips) * 2 + core}
            )

        def all_mate(d):
            src = ag_own if d == 0 else ag_x.at[d - 1]
            return remote(src, ag_c.at[d], agc_s.at[d], agc_r.at[d], {"ctx": mate})

        @pl.loop(1, chips + 1)
        def _(d):
            c = (chip + d) % chips

            @pl.when(has_l)
            def _():
                w_piece(c).wait_recv()

            theirs = medium(2 * c + 1 - core)
            ours = medium(2 * c + core)
            pfb[c] = theirs.astype(BF16)
            to_mate(c).start()
            own[c] = ours

            @pl.when(d > 1)
            def _():
                before = (chip + d - 1) % chips
                to_mate(before).wait_recv()
                sx[d - 2] = (own[before] + rc[before].astype(F32)).astype(BF16)
                to_chip(d - 1).start()
    else:

        @pl.when(has_l)
        def _():
            for h in range(PIECES):
                w_piece(h).wait_recv()

        @pl.loop(0, nc)
        def _(c):
            o_fmr[:, lanes(c)] = medium(c).astype(o_fmr.dtype)

    dot_row = gather(1)
    inv = inv2[...]
    k2[...] = inv * inv * inv * jnp.broadcast_to(dot_row[0:1], (128, 128)).T / D

    @pl.loop(0, nc)
    def _(c):
        for i in range(tiles):
            t = c * tiles + i
            at = pl.ds(i * 128, 128)
            ch = tile(t)
            cs = conv[:, ch]
            q = qs[:, ch].astype(F32)
            mixed = q * cs
            grad_normed = gp[:, ch] * km[:, ch].astype(F32)
            grad_mixed = inv2[...] * (grad_normed * gain[:, ch]) - mixed * k2[...]
            o_qse[:, ch] = (grad_mixed * cs).astype(BF16)
            sm[c, pl.ds(taps, 1), at] = jnp.sum(grad_normed * mixed * inv2[...], axis=0, keepdims=True)
            gcs = (grad_mixed * q).astype(BF16).astype(F32)
            win_gs[t, pl.ds(0, rows), :] = gcs
            for j in range(taps):
                sm[c, pl.ds(j, 1), at] = jnp.sum(gcs * win_se[t, pl.ds(8 - j, rows), :], axis=0, keepdims=True)

    head = remote(win_gs.at[:, pl.ds(0, 8)], win_gs.at[:, pl.ds(rows, 8)], gs_sem.at[0], gs_sem.at[1], {"ctx": left})

    @pl.when(has_l)
    def _():
        head.start()

    if fused:

        def small_to(d):
            return remote(
                sm.at[(me + d) % n], rs_s.at[d - 1], rss_s.at[d - 1], rss_r.at[d - 1], {"ctx": (me + d) % n}
            )

        def small_all(d):
            return remote(
                ag_s.at[0], ag_s.at[d], ags_s.at[d - 1], ags_r.at[d - 1], {"ctx": (me + d) % n}
            )

        for d in range(1, n):
            small_to(d).start()

        to_mate(chip).wait_recv()
        total = own[chip] + rc[chip].astype(F32)
        for d in range(1, chips):
            to_chip(d).wait_recv()
            total = total + rx[d - 1].astype(F32)
        ag_own[...] = total.astype(BF16)
        for d in range(1, chips):
            all_chip(d).start()
        all_mate(0).start()

    @pl.loop(0, PIECES // 2)
    def _(h):
        for i in range(per):
            medium_out(h * per + i)

    if fused:
        total_s = sm[me]
        for d in range(1, n):
            small_to(d).wait_recv()
            total_s = total_s + rs_s[d - 1]
        ag_s[0] = total_s
        for d in range(1, n):
            small_all(d).start()

    @pl.loop(PIECES // 2, PIECES)
    def _(h):
        for i in range(per):
            medium_out(h * per + i)

    if fused:
        for d in range(1, chips):
            all_chip(d).wait_recv()
            all_mate(d).start()

    @pl.when(has_r)
    def _():
        head.wait_recv()

    @pl.loop(0, nc)
    def _(c):
        for i in range(tiles):
            t = c * tiles + i
            ch = tile(t)
            f = fse[:, ch].astype(F32)
            g = win_gs[t, pl.ds(0, rows), :] * f[0:1]
            for j in range(1, taps):
                g = g + win_gs[t, pl.ds(j, rows), :] * f[j : j + 1]
            o_kse[:, ch] = (g * vp[:, ch].astype(F32)).astype(BF16)
            o_val[:, ch] = (g * ks[:, ch].astype(F32)).astype(BF16)

    if fused:
        o_fmr[:, lanes(me)] = ag_own[...]
        for d in range(1, chips):
            o_fmr[:, lanes(((chip + chips - d) % chips) * 2 + core)] = ag_x[d - 1]
        o_small[:, lanes(me)] = ag_s[0]
        for d in range(1, n):
            small_all(d).wait_recv()
            o_small[:, lanes((me + n - d) % n)] = ag_s[d]
        for d in range(chips):
            all_mate(d).wait_recv()
            o_fmr[:, lanes(((chip + chips - d) % chips) * 2 + 1 - core)] = ag_c[d]
        for i in range(chips):
            to_mate(i).wait_send()
            all_mate(i).wait_send()
        for d in range(1, chips):
            to_chip(d).wait_send()
            all_chip(d).wait_send()
        for d in range(1, n):
            small_to(d).wait_send()
            small_all(d).wait_send()
    else:

        @pl.loop(0, nc)
        def _(c):
            o_small[:, lanes(c)] = sm[c]

    @pl.when(has_l)
    def _():
        head.wait_send()

    @pl.when(has_r)
    def _():
        tail.wait_send()
        inv_copy.wait_send()
        for h in range(PIECES):
            w_piece(h).wait_send()


def write_out(val, qse, kse, qmr, kmr, small, gf, *rest):
    outs, (o_fse, o_fmr, o_gain, fse, fmr, gain, sem) = rest[:5], rest[5:]
    copies = [pltpu.make_async_copy(a, b, sem.at[i]) for i, (a, b) in enumerate(zip((val, qse, kse, qmr, kmr), outs))]
    for copy in copies:
        copy.start()
    taps = fse.shape[0]
    part = fmr.shape[0] // 4
    for i in range(4):
        at = pl.ds(i * part, part)
        fmr[at, :] = gf[at, :].astype(F32)
        copies.append(pltpu.make_async_copy(fmr.at[at], o_fmr.at[at], sem.at[5 + i]))
        copies[-1].start()
    fse[...] = small[pl.ds(0, taps), :]
    gain[...] = small[pl.ds(taps, 1), :]
    copies.append(pltpu.make_async_copy(fse, o_fse, sem.at[9]))
    copies.append(pltpu.make_async_copy(gain, o_gain, sem.at[10]))
    copies[-2].start()
    copies[-1].start()
    for copy in copies:
        copy.wait()


def shards(n, ntp, vp, ks, qs, km, qm, og, norm_gain, fse, fmr):
    rows, chans = vp.shape
    taps = fse.shape[0]
    nc = chans // CW
    fused = n == nc and n % 2 == 0
    chips = max(n // 2, 2) if fused else 2
    blk = (rows, CW)
    peers = n if fused else 2
    wide_out = jax.ShapeDtypeStruct((rows, chans), BF16)
    dma = pltpu.SemaphoreType.DMA
    vmem = pltpu.VMEM
    scratch = [vmem((rows, chans), BF16) for _ in range(6)] + [
        vmem((chans,), BF16),
        vmem((1, chans), F32),
        vmem((taps, chans), BF16),
        vmem(fmr.shape, BF16),
        vmem((6, 2 * rows, 2 * rows), BF16),
        dma((10,)),
        vmem((chans // 128, rows + 8, 128), F32),
        vmem((2 * rows, chans), BF16),
        vmem((rows, chans), BF16),
        vmem((rows, chans), BF16),
        vmem((rows, chans), F32),
        vmem((2 * rows, chans), F32),
        vmem((2 * rows, chans), F32),
        vmem((2 * rows, chans), F32),
        vmem((rows, chans), F32),
        vmem((chans // 128, rows + 8, 128), F32),
        vmem((rows, 128), F32),
        vmem((2, 8, 128), F32),
        vmem((2, ntp - 1, 8, 128), F32),
        vmem((8, 128), F32),
        vmem((8, 128), F32),
        vmem((rows, 128), F32),
        vmem((rows, 128), F32),
        vmem((rows, 128), F32),
        vmem((chips,) + blk, BF16),
        vmem((chips,) + blk, F32),
        vmem((chips,) + blk, BF16),
        vmem((chips - 1,) + blk, BF16),
        vmem((chips - 1,) + blk, BF16),
        vmem(blk, BF16),
        vmem((chips - 1,) + blk, BF16),
        vmem((chips,) + blk, BF16),
        vmem((nc, taps + 1, CW), F32),
        vmem((peers - 1, taps + 1, CW), F32),
        vmem((peers, taps + 1, CW), F32),
        dma((2,)),
        dma((PIECES,)), dma((PIECES,)),
        dma((PIECES,)), dma((PIECES,)),
        dma((2, ntp - 1)), dma((2, ntp - 1)),
        dma((2,)),
        dma((2,)),
        dma((chips,)), dma((chips,)),
        dma((chips - 1,)), dma((chips - 1,)),
        dma((chips - 1,)), dma((chips - 1,)),
        dma((chips,)), dma((chips,)),
        dma((peers - 1,)), dma((peers - 1,)),
        dma((peers - 1,)), dma((peers - 1,)),
    ]
    spec = pl.BlockSpec(memory_space=pltpu.VMEM)
    mats = jnp.asarray(matrices(rows))
    operands = (vp, ks, qs, km, qm, og, norm_gain, fse, fmr, mats)
    outs = pl.pallas_call(
        functools.partial(body, n, ntp, fused),
        out_shape=[wide_out] * 5
        + [jax.ShapeDtypeStruct((taps + 1, chans), F32), jax.ShapeDtypeStruct((rows, chans), BF16 if fused else F32)],
        in_specs=[pl.BlockSpec(memory_space=pltpu.HBM)] * 10,
        out_specs=[spec] * 7,
        scratch_shapes=scratch,
        compiler_params=pltpu.CompilerParams(
            collective_id=0, has_side_effects=True, vmem_limit_bytes=40 * 1024 * 1024
        ),
        name="hyena_backward",
    )(*(pltpu.with_memory_space_constraint(x, pltpu.HBM) for x in operands))
    if not fused:
        small, gf = lax.psum(outs[5:], "ctx")
        outs = list(outs[:5]) + [small, gf]
    hbm = pl.BlockSpec(memory_space=pltpu.HBM)
    done = pl.pallas_call(
        write_out,
        out_shape=[wide_out] * 5
        + [
            jax.ShapeDtypeStruct((taps, chans), F32),
            jax.ShapeDtypeStruct((rows, chans), F32),
            jax.ShapeDtypeStruct((1, chans), F32),
        ],
        in_specs=[spec] * 7,
        out_specs=[hbm] * 8,
        scratch_shapes=[vmem((taps, chans), F32), vmem((rows, chans), F32), vmem((1, chans), F32), dma((11,))],
        compiler_params=pltpu.CompilerParams(vmem_limit_bytes=12 * 1024 * 1024),
        name="write_out",
    )(*outs)
    return tuple(done[:7]) + (done[7].reshape(chans),)


def solution(mesh):
    tok = P("ctx", "tp")
    fil = P(None, "tp")
    return jax.shard_map(
        functools.partial(shards, mesh.shape["ctx"], mesh.shape["tp"]),
        mesh=mesh,
        in_specs=(tok,) * 6 + (P("tp"), fil, fil),
        out_specs=(tok,) * 5 + (fil, fil, P("tp")),
        check_vma=False,
    )
```

```python
import functools
import math

import jax
import jax.numpy as jnp
import ml_dtypes
import numpy as np
from jax import lax
from jax.experimental import pallas as pl
from jax.experimental.pallas import tpu as pltpu
from jax.sharding import PartitionSpec as P

D = 8192
CW = 256
PIECES = 4
F32 = jnp.float32
BF16 = jnp.bfloat16


def split(m):
    hi = m.astype(ml_dtypes.bfloat16)
    lo = (m - hi.astype(np.float64)).astype(ml_dtypes.bfloat16)
    return hi, lo


def matrices(rows):
    n = 2 * rows
    theta = 2.0 * math.pi * (np.arange(rows) + 0.5) / n
    ang = theta[:, None] * np.arange(n)[None, :]
    fwd = np.concatenate([np.cos(ang), -np.sin(ang)], axis=0)
    bwd = np.concatenate([np.cos(ang).T, -np.sin(ang).T], axis=1) / rows
    fh, fl = split(fwd)
    near = np.concatenate([fh[:, :rows], fl[:, :rows]], axis=1)
    far = np.concatenate([fh[:, rows:], fl[:, rows:]], axis=1)
    bh, bl = split(bwd)
    first = np.concatenate([bh[:rows], bl[:rows]], axis=0)
    last = np.concatenate([bh[rows:], bl[rows:]], axis=0)
    return np.stack([fh, fl, near, far, first, last])


def body(
    n, ntp, fused,
    vp_h, ks_h, qs_h, km_h, qm_h, og_h, gain_h, fse_h, fmr_h, mats_h,
    o_val, o_qse, o_kse, o_qmr, o_kmr, o_small, o_fmr,
    vp, ks, qs, km, qm, og, gain_in, gain, fse, fmr, mats, in_sem,
    win_se, g2, wsend, wh, conv, fs, os_, xs, gp, win_gs, acc, row_send, row_recv, inv_send, invl_row, inv2, invl2, k2,
    pfb, own, rc, sx, rx, ag_own, ag_x, ag_c, sm, rs_s, ag_s,
    tail_sem, gh_s, gh_r, wh_s, wh_r, row_s, row_r, inv_sem, gs_sem,
    rc_s, rc_r, rx_s, rx_r, agx_s, agx_r, agc_s, agc_r, rss_s, rss_r, ags_s, ags_r,
):
    me = lax.axis_index("ctx")
    tp = lax.axis_index("tp")
    rows, chans = vp.shape
    taps = fse.shape[0]
    nc = chans // CW
    hc = chans // PIECES
    per = hc // CW
    tiles = CW // 128
    has_l = me > 0
    has_r = me < n - 1
    left = (me + n - 1) % n
    right = (me + 1) % n
    mesh_ids = pl.DeviceIdType.MESH

    def remote(src, dst, ssem, rsem, where):
        return pltpu.make_async_remote_copy(
            src_ref=src, dst_ref=dst, send_sem=ssem, recv_sem=rsem, device_id=where, device_id_type=mesh_ids
        )

    def lanes(c):
        return pl.ds(pl.multiple_of(c * CW, CW), CW)

    def tile(t):
        return pl.ds(pl.multiple_of(t * 128, 128), 128)

    def wide(ref):
        return jnp.concatenate([ref[...]] * (CW // 128), axis=1)

    fetch = [
        pltpu.make_async_copy(src, dst, in_sem.at[i])
        for i, (src, dst) in enumerate(
            [(ks_h, ks), (vp_h, vp), (og_h, og), (qm_h, qm), (mats_h, mats), (fmr_h, fmr), (qs_h, qs), (fse_h, fse),
             (gain_h, gain_in), (km_h, km)]
        )
    ]
    for copy in fetch:
        copy.start()

    bar = pltpu.get_barrier_semaphore()
    ctx_peers = [(me + d) % n for d in range(1, n)] if fused else [left, right]
    for p in ctx_peers:
        pl.semaphore_signal(bar, inc=1, device_id={"ctx": p}, device_id_type=mesh_ids)
    for d in range(1, ntp):
        pl.semaphore_signal(bar, inc=1, device_id={"tp": (tp + d) % ntp}, device_id_type=mesh_ids)

    @pl.when(jnp.logical_not(has_l))
    def _():
        win_se[:, pl.ds(0, 8), :] = jnp.zeros((chans // 128, 8, 128), F32)
        wh[...] = jnp.zeros_like(wh)
        invl_row[...] = jnp.zeros_like(invl_row)

    @pl.when(jnp.logical_not(has_r))
    def _():
        g2[pl.ds(rows, rows), :] = jnp.zeros((rows, chans), BF16)
        win_gs[:, pl.ds(rows, 8), :] = jnp.zeros((chans // 128, 8, 128), F32)

    for copy in fetch[:2]:
        copy.wait()

    @pl.loop(0, nc)
    def _(c):
        ch = lanes(c)
        prod = (ks[:, ch].astype(F32) * vp[:, ch].astype(F32)).astype(BF16).astype(F32)
        for i in range(tiles):
            win_se[c * tiles + i, pl.ds(8, rows), :] = prod[:, i * 128 : (i + 1) * 128]

    pl.semaphore_wait(bar, len(ctx_peers) + ntp - 1)

    tail = remote(win_se.at[:, pl.ds(rows, 8)], win_se.at[:, pl.ds(0, 8)], tail_sem.at[0], tail_sem.at[1], {"ctx": right})

    def g_piece(h):
        hl = pl.ds(pl.multiple_of(h * hc, hc), hc)
        return remote(g2.at[pl.ds(0, rows), hl], g2.at[pl.ds(rows, rows), hl], gh_s.at[h], gh_r.at[h], {"ctx": left})

    def w_piece(h):
        hl = pl.ds(pl.multiple_of(h * hc, hc), hc)
        return remote(wsend.at[:, hl], wh.at[:, hl], wh_s.at[h], wh_r.at[h], {"ctx": right})

    @pl.when(has_r)
    def _():
        tail.start()

    for copy in fetch[2:4]:
        copy.wait()

    @pl.loop(0, PIECES)
    def _(h):
        for i in range(per):
            ch = lanes(h * per + i)
            g2[pl.ds(0, rows), ch] = (og[:, ch].astype(F32) * qm[:, ch].astype(F32)).astype(BF16)

        @pl.when(has_l)
        def _():
            g_piece(h).start()

    def twice(x):
        return jnp.concatenate([x, x], axis=0)

    def dot(a, b):
        return jnp.dot(a, b, preferred_element_type=F32)

    def back(re, im, which):
        return dot(mats[which, pl.ds(0, rows), :], jnp.concatenate([re.astype(BF16), im.astype(BF16)], axis=0))

    for copy in fetch[4:6]:
        copy.wait()

    @pl.loop(0, PIECES)
    def _(h):
        for i in range(per):
            ch = lanes(h * per + i)
            fs[:, ch] = dot(mats[2], twice(fmr[:, ch]))
            os_[:, ch] = dot(mats[2], twice(g2[pl.ds(0, rows), ch]))

    @pl.when(has_l)
    def _():
        tail.wait_recv()

    for copy in fetch[6:]:
        copy.wait()
    gain[...] = gain_in[...].astype(F32).reshape(1, chans)
    acc[...] = jnp.zeros_like(acc)

    def fold(x):
        s = x[:, :128]
        for i in range(1, CW // 128):
            s = s + x[:, i * 128 : (i + 1) * 128]
        return s

    @pl.loop(0, PIECES)
    def _(step):
        h = (right // 2 + 1 + step) % PIECES
        for i in range(hc // 128):
            t = h * (hc // 128) + i
            ch = tile(t)
            f = fse[:, ch].astype(F32)
            cs = win_se[t, pl.ds(8, rows), :] * f[0:1]
            for j in range(1, taps):
                cs = cs + win_se[t, pl.ds(8 - j, rows), :] * f[j : j + 1]
            conv[:, ch] = cs
            mixed = qs[:, ch].astype(F32) * cs
            acc[...] += mixed * mixed
            wsend[:, ch] = (mixed * gain[:, ch] * km[:, ch].astype(F32)).astype(BF16)

        @pl.when(has_r)
        def _():
            w_piece(h).start()

    def share(k):
        row_send[k] = jnp.broadcast_to(jnp.sum(acc[...].T, axis=0, keepdims=True), (8, 128))
        for d in range(1, ntp):
            row_copy(k, d).start()

    def row_copy(k, d):
        return remote(
            row_send.at[k], row_recv.at[k, d - 1], row_s.at[k, d - 1], row_r.at[k, d - 1], {"tp": (tp + d) % ntp}
        )

    def gather(k):
        for d in range(1, ntp):
            row_copy(k, d).wait()
        total = row_send[k]
        for d in range(1, ntp):
            total = total + row_recv[k, d - 1]
        return total

    share(0)

    acc[...] = jnp.zeros_like(acc)

    def input_grad(h):
        @pl.when(has_l)
        def _():
            g_piece(h).wait_send()

        @pl.when(has_r)
        def _():
            g_piece(h).wait_recv()

        for i in range(per):
            ch = lanes(h * per + i)
            g = os_[:, ch] + dot(mats[3], twice(g2[pl.ds(rows, rows), ch]))
            gr, gi = g[:rows], g[rows:]
            fr, fi = fs[pl.ds(0, rows), ch], fs[pl.ds(rows, rows), ch]
            grad = back(gr * fr + gi * fi, gi * fr - gr * fi, 4)
            gp[:, ch] = grad
            mixed = qs[:, ch].astype(F32) * conv[:, ch]
            acc[...] += fold(grad * km[:, ch].astype(F32) * gain[:, ch] * mixed)

    pl.loop(0, PIECES // 2)(input_grad)

    inv_row = lax.rsqrt(gather(0) / D + 1e-06)
    inv_send[...] = inv_row
    inv_copy = remote(inv_send, invl_row, inv_sem.at[0], inv_sem.at[1], {"ctx": right})

    @pl.when(has_r)
    def _():
        inv_copy.start()

    inv2[...] = jnp.broadcast_to(inv_row[0:1], (128, 128)).T

    pl.loop(PIECES // 2, PIECES)(input_grad)

    share(1)

    @pl.when(has_l)
    def _():
        inv_copy.wait_recv()

    invl2[...] = jnp.broadcast_to(invl_row[0:1], (128, 128)).T

    def medium(c):
        ch = lanes(c)
        kmf = km[:, ch].astype(F32)
        mixed = qs[:, ch].astype(F32) * conv[:, ch]
        normed = (mixed * wide(inv2) * gain[:, ch]).astype(BF16)
        prod = (kmf * normed.astype(F32)).astype(BF16)
        halo = (wh[:, ch].astype(F32) * wide(invl2)).astype(BF16)
        window = jnp.concatenate([halo, prod], axis=0)
        o_kmr[:, ch] = (gp[:, ch] * normed.astype(F32)).astype(BF16)
        x = dot(mats[0], window)
        xr, xi = x[:rows], x[rows:]
        xs[:, ch] = x
        gr, gi = os_[pl.ds(0, rows), ch], os_[pl.ds(rows, rows), ch]
        return -back(gr * xr + gi * xi, gi * xr - gr * xi, 5)

    def medium_out(c):
        ch = lanes(c)
        xr, xi = xs[pl.ds(0, rows), ch], xs[pl.ds(rows, rows), ch]
        fr, fi = fs[pl.ds(0, rows), ch], fs[pl.ds(rows, rows), ch]
        y = back(xr * fr - xi * fi, xr * fi + xi * fr, 5)
        o_qmr[:, ch] = (og[:, ch].astype(F32) * y).astype(BF16)

    if fused:
        chips = n // 2
        core = me % 2
        chip = me // 2
        mate = me + 1 - 2 * core

        def to_mate(i):
            return remote(pfb.at[i], rc.at[i], rc_s.at[i], rc_r.at[i], {"ctx": mate})

        def to_chip(d):
            return remote(
                sx.at[d - 1], rx.at[d - 1], rx_s.at[d - 1], rx_r.at[d - 1], {"ctx": ((chip + d) % chips) * 2 + core}
            )

        def all_chip(d):
            return remote(
                ag_own, ag_x.at[d - 1], agx_s.at[d - 1], agx_r.at[d - 1], {"ctx": ((chip + d) % chips) * 2 + core}
            )

        def all_mate(d):
            src = ag_own if d == 0 else ag_x.at[d - 1]
            return remote(src, ag_c.at[d], agc_s.at[d], agc_r.at[d], {"ctx": mate})

        @pl.loop(1, chips + 1)
        def _(d):
            c = (chip + d) % chips

            @pl.when(has_l)
            def _():
                w_piece(c).wait_recv()

            theirs = medium(2 * c + 1 - core)
            ours = medium(2 * c + core)
            pfb[c] = theirs.astype(BF16)
            to_mate(c).start()
            own[c] = ours

            @pl.when(d > 1)
            def _():
                before = (chip + d - 1) % chips
                to_mate(before).wait_recv()
                sx[d - 2] = (own[before] + rc[before].astype(F32)).astype(BF16)
                to_chip(d - 1).start()
    else:

        @pl.when(has_l)
        def _():
            for h in range(PIECES):
                w_piece(h).wait_recv()

        @pl.loop(0, nc)
        def _(c):
            o_fmr[:, lanes(c)] = medium(c).astype(o_fmr.dtype)

    dot_row = gather(1)
    inv = inv2[...]
    k2[...] = inv * inv * inv * jnp.broadcast_to(dot_row[0:1], (128, 128)).T / D

    @pl.loop(0, nc)
    def _(c):
        for i in range(tiles):
            t = c * tiles + i
            at = pl.ds(i * 128, 128)
            ch = tile(t)
            cs = conv[:, ch]
            q = qs[:, ch].astype(F32)
            mixed = q * cs
            grad_normed = gp[:, ch] * km[:, ch].astype(F32)
            grad_mixed = inv2[...] * (grad_normed * gain[:, ch]) - mixed * k2[...]
            o_qse[:, ch] = (grad_mixed * cs).astype(BF16)
            sm[c, pl.ds(taps, 1), at] = jnp.sum(grad_normed * mixed * inv2[...], axis=0, keepdims=True)
            gcs = (grad_mixed * q).astype(BF16).astype(F32)
            win_gs[t, pl.ds(0, rows), :] = gcs
            for j in range(taps):
                sm[c, pl.ds(j, 1), at] = jnp.sum(gcs * win_se[t, pl.ds(8 - j, rows), :], axis=0, keepdims=True)

    head = remote(win_gs.at[:, pl.ds(0, 8)], win_gs.at[:, pl.ds(rows, 8)], gs_sem.at[0], gs_sem.at[1], {"ctx": left})

    @pl.when(has_l)
    def _():
        head.start()

    if fused:

        def small_to(d):
            return remote(
                sm.at[(me + d) % n], rs_s.at[d - 1], rss_s.at[d - 1], rss_r.at[d - 1], {"ctx": (me + d) % n}
            )

        def small_all(d):
            return remote(
                ag_s.at[0], ag_s.at[d], ags_s.at[d - 1], ags_r.at[d - 1], {"ctx": (me + d) % n}
            )

        for d in range(1, n):
            small_to(d).start()

        to_mate(chip).wait_recv()
        total = own[chip] + rc[chip].astype(F32)
        for d in range(1, chips):
            to_chip(d).wait_recv()
            total = total + rx[d - 1].astype(F32)
        ag_own[...] = total.astype(BF16)
        for d in range(1, chips):
            all_chip(d).start()
        all_mate(0).start()

    @pl.loop(0, PIECES // 2)
    def _(h):
        for i in range(per):
            medium_out(h * per + i)

    if fused:
        total_s = sm[me]
        for d in range(1, n):
            small_to(d).wait_recv()
            total_s = total_s + rs_s[d - 1]
        ag_s[0] = total_s
        for d in range(1, n):
            small_all(d).start()

    @pl.loop(PIECES // 2, PIECES)
    def _(h):
        for i in range(per):
            medium_out(h * per + i)

    if fused:
        for d in range(1, chips):
            all_chip(d).wait_recv()
            all_mate(d).start()

    @pl.when(has_r)
    def _():
        head.wait_recv()

    @pl.loop(0, nc)
    def _(c):
        for i in range(tiles):
            t = c * tiles + i
            ch = tile(t)
            f = fse[:, ch].astype(F32)
            g = win_gs[t, pl.ds(0, rows), :] * f[0:1]
            for j in range(1, taps):
                g = g + win_gs[t, pl.ds(j, rows), :] * f[j : j + 1]
            o_kse[:, ch] = (g * vp[:, ch].astype(F32)).astype(BF16)
            o_val[:, ch] = (g * ks[:, ch].astype(F32)).astype(BF16)

    if fused:
        o_fmr[:, lanes(me)] = ag_own[...]
        for d in range(1, chips):
            o_fmr[:, lanes(((chip + chips - d) % chips) * 2 + core)] = ag_x[d - 1]
        o_small[:, lanes(me)] = ag_s[0]
        for d in range(1, n):
            small_all(d).wait_recv()
            o_small[:, lanes((me + n - d) % n)] = ag_s[d]
        for d in range(chips):
            all_mate(d).wait_recv()
            o_fmr[:, lanes(((chip + chips - d) % chips) * 2 + 1 - core)] = ag_c[d]
        for i in range(chips):
            to_mate(i).wait_send()
            all_mate(i).wait_send()
        for d in range(1, chips):
            to_chip(d).wait_send()
            all_chip(d).wait_send()
        for d in range(1, n):
            small_to(d).wait_send()
            small_all(d).wait_send()
    else:

        @pl.loop(0, nc)
        def _(c):
            o_small[:, lanes(c)] = sm[c]

    @pl.when(has_l)
    def _():
        head.wait_send()

    @pl.when(has_r)
    def _():
        tail.wait_send()
        inv_copy.wait_send()
        for h in range(PIECES):
            w_piece(h).wait_send()


def write_out(val, qse, kse, qmr, kmr, small, gf, *rest):
    outs, (o_fse, o_fmr, o_gain, fse, fmr, gain, sem) = rest[:5], rest[5:]
    copies = [pltpu.make_async_copy(a, b, sem.at[i]) for i, (a, b) in enumerate(zip((val, qse, kse, qmr, kmr), outs))]
    for copy in copies:
        copy.start()
    taps = fse.shape[0]
    part = fmr.shape[0] // 4
    for i in range(4):
        at = pl.ds(i * part, part)
        fmr[at, :] = gf[at, :].astype(F32)
        copies.append(pltpu.make_async_copy(fmr.at[at], o_fmr.at[at], sem.at[5 + i]))
        copies[-1].start()
    fse[...] = small[pl.ds(0, taps), :]
    gain[...] = small[pl.ds(taps, 1), :]
    copies.append(pltpu.make_async_copy(fse, o_fse, sem.at[9]))
    copies.append(pltpu.make_async_copy(gain, o_gain, sem.at[10]))
    copies[-2].start()
    copies[-1].start()
    for copy in copies:
        copy.wait()


def shards(n, ntp, vp, ks, qs, km, qm, og, norm_gain, fse, fmr):
    rows, chans = vp.shape
    taps = fse.shape[0]
    nc = chans // CW
    fused = n == nc and n % 2 == 0
    chips = max(n // 2, 2) if fused else 2
    blk = (rows, CW)
    peers = n if fused else 2
    wide_out = jax.ShapeDtypeStruct((rows, chans), BF16)
    dma = pltpu.SemaphoreType.DMA
    vmem = pltpu.VMEM
    scratch = [vmem((rows, chans), BF16) for _ in range(6)] + [
        vmem((chans,), BF16),
        vmem((1, chans), F32),
        vmem((taps, chans), BF16),
        vmem(fmr.shape, BF16),
        vmem((6, 2 * rows, 2 * rows), BF16),
        dma((10,)),
        vmem((chans // 128, rows + 8, 128), F32),
        vmem((2 * rows, chans), BF16),
        vmem((rows, chans), BF16),
        vmem((rows, chans), BF16),
        vmem((rows, chans), F32),
        vmem((2 * rows, chans), F32),
        vmem((2 * rows, chans), F32),
        vmem((2 * rows, chans), F32),
        vmem((rows, chans), F32),
        vmem((chans // 128, rows + 8, 128), F32),
        vmem((rows, 128), F32),
        vmem((2, 8, 128), F32),
        vmem((2, ntp - 1, 8, 128), F32),
        vmem((8, 128), F32),
        vmem((8, 128), F32),
        vmem((rows, 128), F32),
        vmem((rows, 128), F32),
        vmem((rows, 128), F32),
        vmem((chips,) + blk, BF16),
        vmem((chips,) + blk, F32),
        vmem((chips,) + blk, BF16),
        vmem((chips - 1,) + blk, BF16),
        vmem((chips - 1,) + blk, BF16),
        vmem(blk, BF16),
        vmem((chips - 1,) + blk, BF16),
        vmem((chips,) + blk, BF16),
        vmem((nc, taps + 1, CW), F32),
        vmem((peers - 1, taps + 1, CW), F32),
        vmem((peers, taps + 1, CW), F32),
        dma((2,)),
        dma((PIECES,)), dma((PIECES,)),
        dma((PIECES,)), dma((PIECES,)),
        dma((2, ntp - 1)), dma((2, ntp - 1)),
        dma((2,)),
        dma((2,)),
        dma((chips,)), dma((chips,)),
        dma((chips - 1,)), dma((chips - 1,)),
        dma((chips - 1,)), dma((chips - 1,)),
        dma((chips,)), dma((chips,)),
        dma((peers - 1,)), dma((peers - 1,)),
        dma((peers - 1,)), dma((peers - 1,)),
    ]
    spec = pl.BlockSpec(memory_space=pltpu.VMEM)
    mats = jnp.asarray(matrices(rows))
    operands = (vp, ks, qs, km, qm, og, norm_gain, fse, fmr, mats)
    outs = pl.pallas_call(
        functools.partial(body, n, ntp, fused),
        out_shape=[wide_out] * 5
        + [jax.ShapeDtypeStruct((taps + 1, chans), F32), jax.ShapeDtypeStruct((rows, chans), BF16 if fused else F32)],
        in_specs=[pl.BlockSpec(memory_space=pltpu.HBM)] * 10,
        out_specs=[spec] * 7,
        scratch_shapes=scratch,
        compiler_params=pltpu.CompilerParams(
            collective_id=0, has_side_effects=True, vmem_limit_bytes=40 * 1024 * 1024
        ),
        name="hyena_backward",
    )(*(pltpu.with_memory_space_constraint(x, pltpu.HBM) for x in operands))
    if not fused:
        small, gf = lax.psum(outs[5:], "ctx")
        outs = list(outs[:5]) + [small, gf]
    hbm = pl.BlockSpec(memory_space=pltpu.HBM)
    done = pl.pallas_call(
        write_out,
        out_shape=[wide_out] * 5
        + [
            jax.ShapeDtypeStruct((taps, chans), F32),
            jax.ShapeDtypeStruct((rows, chans), F32),
            jax.ShapeDtypeStruct((1, chans), F32),
        ],
        in_specs=[spec] * 7,
        out_specs=[hbm] * 8,
        scratch_shapes=[vmem((taps, chans), F32), vmem((rows, chans), F32), vmem((1, chans), F32), dma((11,))],
        compiler_params=pltpu.CompilerParams(vmem_limit_bytes=12 * 1024 * 1024),
        name="write_out",
    )(*outs)
    return tuple(done[:7]) + (done[7].reshape(chans),)


def solution(mesh):
    tok = P("ctx", "tp")
    fil = P(None, "tp")
    return jax.shard_map(
        functools.partial(shards, mesh.shape["ctx"], mesh.shape["tp"]),
        mesh=mesh,
        in_specs=(tok,) * 6 + (P("tp"), fil, fil),
        out_specs=(tok,) * 5 + (fil, fil, P("tp")),
        check_vma=False,
    )
```

```python
import functools
import math

import jax
import jax.numpy as jnp
import ml_dtypes
import numpy as np
from jax import lax
from jax.experimental import pallas as pl
from jax.experimental.pallas import tpu as pltpu
from jax.sharding import PartitionSpec as P

D = 8192
CW = 256
PIECES = 4
F32 = jnp.float32
BF16 = jnp.bfloat16


def split(m):
    hi = m.astype(ml_dtypes.bfloat16)
    lo = (m - hi.astype(np.float64)).astype(ml_dtypes.bfloat16)
    return hi, lo


def matrices(rows):
    n = 2 * rows
    theta = 2.0 * math.pi * (np.arange(rows) + 0.5) / n
    ang = theta[:, None] * np.arange(n)[None, :]
    fwd = np.concatenate([np.cos(ang), -np.sin(ang)], axis=0)
    bwd = np.concatenate([np.cos(ang).T, -np.sin(ang).T], axis=1) / rows
    fh, fl = split(fwd)
    near = np.concatenate([fh[:, :rows], fl[:, :rows]], axis=1)
    bh = bwd.astype(ml_dtypes.bfloat16)
    return np.stack([fh, near, bh])


def body(
    n, ntp, fused,
    vp_h, ks_h, qs_h, km_h, qm_h, og_h, gain_h, fse_h, fmr_h, mats_h,
    o_val, o_qse, o_kse, o_qmr, o_kmr, o_small, o_fmr,
    vp, ks, qs, km, qm, og, gain_in, gain, fse, fmr, mats, in_sem,
    win_se, g2, wsend, wh, conv, fs, gs, gp, win_gs, acc, row_send, row_recv, inv2, k2,
    pfb, own, rc, sx, rx, ag_own, ag_x, ag_c, sm, rs_s, ag_s,
    tail_sem, gh_s, gh_r, wh_s, wh_r, row_s, row_r, gs_sem,
    rc_s, rc_r, rx_s, rx_r, agx_s, agx_r, agc_s, agc_r, rss_s, rss_r, ags_s, ags_r,
):
    me = lax.axis_index("ctx")
    tp = lax.axis_index("tp")
    rows, chans = vp.shape
    taps = fse.shape[0]
    nc = chans // CW
    hc = chans // PIECES
    per = hc // CW
    tiles = CW // 128
    has_l = me > 0
    has_r = me < n - 1
    left = (me + n - 1) % n
    right = (me + 1) % n
    mesh_ids = pl.DeviceIdType.MESH

    def remote(src, dst, ssem, rsem, where):
        return pltpu.make_async_remote_copy(
            src_ref=src, dst_ref=dst, send_sem=ssem, recv_sem=rsem, device_id=where, device_id_type=mesh_ids
        )

    def lanes(c):
        return pl.ds(pl.multiple_of(c * CW, CW), CW)

    def tile(t):
        return pl.ds(pl.multiple_of(t * 128, 128), 128)

    def wide(ref):
        return jnp.concatenate([ref[...]] * (CW // 128), axis=1)

    fetch = [
        pltpu.make_async_copy(src, dst, in_sem.at[i])
        for i, (src, dst) in enumerate(
            [(ks_h, ks), (vp_h, vp), (og_h, og), (qm_h, qm), (mats_h, mats), (fmr_h, fmr), (qs_h, qs), (fse_h, fse),
             (gain_h, gain_in), (km_h, km)]
        )
    ]
    for copy in fetch:
        copy.start()

    bar = pltpu.get_barrier_semaphore()
    ctx_peers = [(me + d) % n for d in range(1, n)] if fused else [left, right]
    for p in ctx_peers:
        pl.semaphore_signal(bar, inc=1, device_id={"ctx": p}, device_id_type=mesh_ids)
    for d in range(1, ntp):
        pl.semaphore_signal(bar, inc=1, device_id={"tp": (tp + d) % ntp}, device_id_type=mesh_ids)

    @pl.when(jnp.logical_not(has_l))
    def _():
        win_se[:, pl.ds(0, 8), :] = jnp.zeros((chans // 128, 8, 128), F32)
        wh[...] = jnp.zeros_like(wh)

    @pl.when(jnp.logical_not(has_r))
    def _():
        g2[pl.ds(rows, rows), :] = jnp.zeros((rows, chans), BF16)
        win_gs[:, pl.ds(rows, 8), :] = jnp.zeros((chans // 128, 8, 128), F32)

    for copy in fetch[:2]:
        copy.wait()

    @pl.loop(0, nc)
    def _(c):
        ch = lanes(c)
        prod = (ks[:, ch].astype(F32) * vp[:, ch].astype(F32)).astype(BF16).astype(F32)
        for i in range(tiles):
            win_se[c * tiles + i, pl.ds(8, rows), :] = prod[:, i * 128 : (i + 1) * 128]

    pl.semaphore_wait(bar, len(ctx_peers) + ntp - 1)

    tail = remote(win_se.at[:, pl.ds(rows, 8)], win_se.at[:, pl.ds(0, 8)], tail_sem.at[0], tail_sem.at[1], {"ctx": right})

    def g_piece(h):
        hl = pl.ds(pl.multiple_of(h * hc, hc), hc)
        return remote(g2.at[pl.ds(0, rows), hl], g2.at[pl.ds(rows, rows), hl], gh_s.at[h], gh_r.at[h], {"ctx": left})

    def w_piece(h):
        hl = pl.ds(pl.multiple_of(h * hc, hc), hc)
        return remote(wsend.at[:, hl], wh.at[:, hl], wh_s.at[h], wh_r.at[h], {"ctx": right})

    @pl.when(has_r)
    def _():
        tail.start()

    for copy in fetch[2:4]:
        copy.wait()

    @pl.loop(0, PIECES)
    def _(h):
        for i in range(per):
            ch = lanes(h * per + i)
            g2[pl.ds(0, rows), ch] = (og[:, ch].astype(F32) * qm[:, ch].astype(F32)).astype(BF16)

        @pl.when(has_l)
        def _():
            g_piece(h).start()

    def twice(x):
        return jnp.concatenate([x, x], axis=0)

    def dot(a, b):
        return jnp.dot(a, b, preferred_element_type=F32)

    def back(re, im, at):
        return dot(mats[2, pl.ds(at, rows), :], jnp.concatenate([re.astype(BF16), im.astype(BF16)], axis=0))

    for copy in fetch[4:6]:
        copy.wait()

    @pl.loop(0, PIECES)
    def _(h):
        for i in range(per):
            ch = lanes(h * per + i)
            fs[:, ch] = dot(mats[1], twice(fmr[:, ch]))

    @pl.when(has_l)
    def _():
        tail.wait_recv()

    for copy in fetch[6:]:
        copy.wait()
    gain[...] = gain_in[...].astype(F32).reshape(1, chans)
    acc[...] = jnp.zeros_like(acc)

    def fold(x):
        s = x[:, :128]
        for i in range(1, CW // 128):
            s = s + x[:, i * 128 : (i + 1) * 128]
        return s

    @pl.loop(0, PIECES)
    def _(h):
        for i in range(hc // 128):
            t = h * (hc // 128) + i
            ch = tile(t)
            f = fse[:, ch].astype(F32)
            cs = win_se[t, pl.ds(8, rows), :] * f[0:1]
            for j in range(1, taps):
                cs = cs + win_se[t, pl.ds(8 - j, rows), :] * f[j : j + 1]
            conv[:, ch] = cs
            mixed = qs[:, ch].astype(F32) * cs
            acc[...] += mixed * mixed

    def share(k):
        row_send[k] = jnp.broadcast_to(jnp.sum(acc[...].T, axis=0, keepdims=True), (8, 128))
        for d in range(1, ntp):
            row_copy(k, d).start()

    def row_copy(k, d):
        return remote(
            row_send.at[k], row_recv.at[k, d - 1], row_s.at[k, d - 1], row_r.at[k, d - 1], {"tp": (tp + d) % ntp}
        )

    def gather(k):
        for d in range(1, ntp):
            row_copy(k, d).wait()
        total = row_send[k]
        for d in range(1, ntp):
            total = total + row_recv[k, d - 1]
        return total

    share(0)

    acc[...] = jnp.zeros_like(acc)

    def input_grad(h):
        @pl.when(has_l)
        def _():
            g_piece(h).wait_send()

        @pl.when(has_r)
        def _():
            g_piece(h).wait_recv()

        for i in range(per):
            ch = lanes(h * per + i)
            g = dot(mats[0], g2[:, ch])
            gs[:, ch] = g
            gr, gi = g[:rows], g[rows:]
            fr, fi = fs[pl.ds(0, rows), ch], fs[pl.ds(rows, rows), ch]
            grad = back(gr * fr + gi * fi, gi * fr - gr * fi, 0)
            gp[:, ch] = grad
            mixed = qs[:, ch].astype(F32) * conv[:, ch]
            acc[...] += fold(grad * km[:, ch].astype(F32) * gain[:, ch] * mixed)

    pl.loop(0, PIECES)(input_grad)
    share(1)

    inv_row = lax.rsqrt(gather(0) / D + 1e-06)
    inv2[...] = jnp.broadcast_to(inv_row[0:1], (128, 128)).T

    def medium(c):
        ch = lanes(c)
        mixed = qs[:, ch].astype(F32) * conv[:, ch]
        normed = (mixed * wide(inv2) * gain[:, ch]).astype(BF16).astype(F32)
        prod = (km[:, ch].astype(F32) * normed).astype(BF16)
        wsend[:, ch] = prod
        o_kmr[:, ch] = (gp[:, ch] * normed).astype(BF16)
        x = dot(mats[1], twice(prod))
        xr, xi = x[:rows], x[rows:]
        gr, gi = gs[pl.ds(0, rows), ch], gs[pl.ds(rows, rows), ch]
        return back(gr * xr + gi * xi, gi * xr - gr * xi, 0)

    def medium_out(c):
        ch = lanes(c)
        x = dot(mats[0], jnp.concatenate([wh[:, ch], wsend[:, ch]], axis=0))
        xr, xi = x[:rows], x[rows:]
        fr, fi = fs[pl.ds(0, rows), ch], fs[pl.ds(rows, rows), ch]
        y = back(xr * fr - xi * fi, xr * fi + xi * fr, rows)
        o_qmr[:, ch] = (og[:, ch].astype(F32) * y).astype(BF16)

    if fused:
        chips = n // 2
        core = me % 2
        chip = me // 2
        mate = me + 1 - 2 * core

        def to_mate(i):
            return remote(pfb.at[i], rc.at[i], rc_s.at[i], rc_r.at[i], {"ctx": mate})

        def to_chip(d):
            return remote(
                sx.at[d - 1], rx.at[d - 1], rx_s.at[d - 1], rx_r.at[d - 1], {"ctx": ((chip + d) % chips) * 2 + core}
            )

        def all_chip(d):
            return remote(
                ag_own, ag_x.at[d - 1], agx_s.at[d - 1], agx_r.at[d - 1], {"ctx": ((chip + d) % chips) * 2 + core}
            )

        def all_mate(d):
            src = ag_own if d == 0 else ag_x.at[d - 1]
            return remote(src, ag_c.at[d], agc_s.at[d], agc_r.at[d], {"ctx": mate})

        @pl.loop(1, chips + 1)
        def _(d):
            c = (chip + d) % chips

            theirs = medium(2 * c + 1 - core)
            ours = medium(2 * c + core)
            pfb[c] = theirs.astype(BF16)
            to_mate(c).start()
            own[c] = ours

            @pl.when(has_r)
            def _():
                w_piece(c).start()

            @pl.when(d > 1)
            def _():
                before = (chip + d - 1) % chips
                to_mate(before).wait_recv()
                sx[d - 2] = (own[before] + rc[before].astype(F32)).astype(BF16)
                to_chip(d - 1).start()
    else:

        @pl.loop(0, PIECES)
        def _(h):
            for i in range(per):
                c = h * per + i
                o_fmr[:, lanes(c)] = medium(c).astype(o_fmr.dtype)

            @pl.when(has_r)
            def _():
                w_piece(h).start()

    dot_row = gather(1)
    inv = inv2[...]
    k2[...] = inv * inv * inv * jnp.broadcast_to(dot_row[0:1], (128, 128)).T / D

    @pl.loop(0, nc)
    def _(c):
        for i in range(tiles):
            t = c * tiles + i
            at = pl.ds(i * 128, 128)
            ch = tile(t)
            cs = conv[:, ch]
            q = qs[:, ch].astype(F32)
            mixed = q * cs
            grad_normed = gp[:, ch] * km[:, ch].astype(F32)
            grad_mixed = inv2[...] * (grad_normed * gain[:, ch]) - mixed * k2[...]
            o_qse[:, ch] = (grad_mixed * cs).astype(BF16)
            sm[c, pl.ds(taps, 1), at] = jnp.sum(grad_normed * mixed * inv2[...], axis=0, keepdims=True)
            gcs = (grad_mixed * q).astype(BF16).astype(F32)
            win_gs[t, pl.ds(0, rows), :] = gcs
            for j in range(taps):
                sm[c, pl.ds(j, 1), at] = jnp.sum(gcs * win_se[t, pl.ds(8 - j, rows), :], axis=0, keepdims=True)

    head = remote(win_gs.at[:, pl.ds(0, 8)], win_gs.at[:, pl.ds(rows, 8)], gs_sem.at[0], gs_sem.at[1], {"ctx": left})

    @pl.when(has_l)
    def _():
        head.start()

    if fused:

        def small_to(d):
            return remote(
                sm.at[(me + d) % n], rs_s.at[d - 1], rss_s.at[d - 1], rss_r.at[d - 1], {"ctx": (me + d) % n}
            )

        def small_all(d):
            return remote(
                ag_s.at[0], ag_s.at[d], ags_s.at[d - 1], ags_r.at[d - 1], {"ctx": (me + d) % n}
            )

        for d in range(1, n):
            small_to(d).start()

        to_mate(chip).wait_recv()
        total = own[chip] + rc[chip].astype(F32)
        for d in range(1, chips):
            to_chip(d).wait_recv()
            total = total + rx[d - 1].astype(F32)
        ag_own[...] = total.astype(BF16)
        for d in range(1, chips):
            all_chip(d).start()
        all_mate(0).start()

    def medium_piece(step):
        h = (left // 2 + 1 + step) % PIECES

        @pl.when(has_l)
        def _():
            w_piece(h).wait_recv()

        for i in range(per):
            medium_out(h * per + i)

    pl.loop(0, PIECES // 2)(medium_piece)

    if fused:
        total_s = sm[me]
        for d in range(1, n):
            small_to(d).wait_recv()
            total_s = total_s + rs_s[d - 1]
        ag_s[0] = total_s
        for d in range(1, n):
            small_all(d).start()

    pl.loop(PIECES // 2, PIECES)(medium_piece)

    if fused:
        for d in range(1, chips):
            all_chip(d).wait_recv()
            all_mate(d).start()

    @pl.when(has_r)
    def _():
        head.wait_recv()

    @pl.loop(0, nc)
    def _(c):
        for i in range(tiles):
            t = c * tiles + i
            ch = tile(t)
            f = fse[:, ch].astype(F32)
            g = win_gs[t, pl.ds(0, rows), :] * f[0:1]
            for j in range(1, taps):
                g = g + win_gs[t, pl.ds(j, rows), :] * f[j : j + 1]
            o_kse[:, ch] = (g * vp[:, ch].astype(F32)).astype(BF16)
            o_val[:, ch] = (g * ks[:, ch].astype(F32)).astype(BF16)

    if fused:
        o_fmr[:, lanes(me)] = ag_own[...]
        for d in range(1, chips):
            o_fmr[:, lanes(((chip + chips - d) % chips) * 2 + core)] = ag_x[d - 1]
        o_small[:, lanes(me)] = ag_s[0]
        for d in range(1, n):
            small_all(d).wait_recv()
            o_small[:, lanes((me + n - d) % n)] = ag_s[d]
        for d in range(chips):
            all_mate(d).wait_recv()
            o_fmr[:, lanes(((chip + chips - d) % chips) * 2 + 1 - core)] = ag_c[d]
        for i in range(chips):
            to_mate(i).wait_send()
            all_mate(i).wait_send()
        for d in range(1, chips):
            to_chip(d).wait_send()
            all_chip(d).wait_send()
        for d in range(1, n):
            small_to(d).wait_send()
            small_all(d).wait_send()
    else:

        @pl.loop(0, nc)
        def _(c):
            o_small[:, lanes(c)] = sm[c]

    @pl.when(has_l)
    def _():
        head.wait_send()

    @pl.when(has_r)
    def _():
        tail.wait_send()
        for h in range(PIECES):
            w_piece(h).wait_send()


def write_out(val, qse, kse, qmr, kmr, small, gf, *rest):
    outs, (o_fse, o_fmr, o_gain, fse, fmr, gain, sem) = rest[:5], rest[5:]
    copies = [pltpu.make_async_copy(a, b, sem.at[i]) for i, (a, b) in enumerate(zip((val, qse, kse, qmr, kmr), outs))]
    for copy in copies:
        copy.start()
    taps = fse.shape[0]
    part = fmr.shape[0] // 4
    for i in range(4):
        at = pl.ds(i * part, part)
        fmr[at, :] = gf[at, :].astype(F32)
        copies.append(pltpu.make_async_copy(fmr.at[at], o_fmr.at[at], sem.at[5 + i]))
        copies[-1].start()
    fse[...] = small[pl.ds(0, taps), :]
    gain[...] = small[pl.ds(taps, 1), :]
    copies.append(pltpu.make_async_copy(fse, o_fse, sem.at[9]))
    copies.append(pltpu.make_async_copy(gain, o_gain, sem.at[10]))
    copies[-2].start()
    copies[-1].start()
    for copy in copies:
        copy.wait()


def shards(n, ntp, vp, ks, qs, km, qm, og, norm_gain, fse, fmr):
    rows, chans = vp.shape
    taps = fse.shape[0]
    nc = chans // CW
    fused = n == nc and n % 2 == 0
    chips = max(n // 2, 2) if fused else 2
    blk = (rows, CW)
    peers = n if fused else 2
    wide_out = jax.ShapeDtypeStruct((rows, chans), BF16)
    dma = pltpu.SemaphoreType.DMA
    vmem = pltpu.VMEM
    scratch = [vmem((rows, chans), BF16) for _ in range(6)] + [
        vmem((chans,), BF16),
        vmem((1, chans), F32),
        vmem((taps, chans), BF16),
        vmem(fmr.shape, BF16),
        vmem((3, 2 * rows, 2 * rows), BF16),
        dma((10,)),
        vmem((chans // 128, rows + 8, 128), F32),
        vmem((2 * rows, chans), BF16),
        vmem((rows, chans), BF16),
        vmem((rows, chans), BF16),
        vmem((rows, chans), F32),
        vmem((2 * rows, chans), F32),
        vmem((2 * rows, chans), F32),
        vmem((rows, chans), F32),
        vmem((chans // 128, rows + 8, 128), F32),
        vmem((rows, 128), F32),
        vmem((2, 8, 128), F32),
        vmem((2, ntp - 1, 8, 128), F32),
        vmem((rows, 128), F32),
        vmem((rows, 128), F32),
        vmem((chips,) + blk, BF16),
        vmem((chips,) + blk, F32),
        vmem((chips,) + blk, BF16),
        vmem((chips - 1,) + blk, BF16),
        vmem((chips - 1,) + blk, BF16),
        vmem(blk, BF16),
        vmem((chips - 1,) + blk, BF16),
        vmem((chips,) + blk, BF16),
        vmem((nc, taps + 1, CW), F32),
        vmem((peers - 1, taps + 1, CW), F32),
        vmem((peers, taps + 1, CW), F32),
        dma((2,)),
        dma((PIECES,)), dma((PIECES,)),
        dma((PIECES,)), dma((PIECES,)),
        dma((2, ntp - 1)), dma((2, ntp - 1)),
        dma((2,)),
        dma((chips,)), dma((chips,)),
        dma((chips - 1,)), dma((chips - 1,)),
        dma((chips - 1,)), dma((chips - 1,)),
        dma((chips,)), dma((chips,)),
        dma((peers - 1,)), dma((peers - 1,)),
        dma((peers - 1,)), dma((peers - 1,)),
    ]
    spec = pl.BlockSpec(memory_space=pltpu.VMEM)
    mats = jnp.asarray(matrices(rows))
    operands = (vp, ks, qs, km, qm, og, norm_gain, fse, fmr, mats)
    outs = pl.pallas_call(
        functools.partial(body, n, ntp, fused),
        out_shape=[wide_out] * 5
        + [jax.ShapeDtypeStruct((taps + 1, chans), F32), jax.ShapeDtypeStruct((rows, chans), BF16 if fused else F32)],
        in_specs=[pl.BlockSpec(memory_space=pltpu.HBM)] * 10,
        out_specs=[spec] * 7,
        scratch_shapes=scratch,
        compiler_params=pltpu.CompilerParams(
            collective_id=0, has_side_effects=True, vmem_limit_bytes=40 * 1024 * 1024
        ),
        name="hyena_backward",
    )(*(pltpu.with_memory_space_constraint(x, pltpu.HBM) for x in operands))
    if not fused:
        small, gf = lax.psum(outs[5:], "ctx")
        outs = list(outs[:5]) + [small, gf]
    hbm = pl.BlockSpec(memory_space=pltpu.HBM)
    done = pl.pallas_call(
        write_out,
        out_shape=[wide_out] * 5
        + [
            jax.ShapeDtypeStruct((taps, chans), F32),
            jax.ShapeDtypeStruct((rows, chans), F32),
            jax.ShapeDtypeStruct((1, chans), F32),
        ],
        in_specs=[spec] * 7,
        out_specs=[hbm] * 8,
        scratch_shapes=[vmem((taps, chans), F32), vmem((rows, chans), F32), vmem((1, chans), F32), dma((11,))],
        compiler_params=pltpu.CompilerParams(vmem_limit_bytes=12 * 1024 * 1024),
        name="write_out",
    )(*outs)
    return tuple(done[:7]) + (done[7].reshape(chans),)


def solution(mesh):
    tok = P("ctx", "tp")
    fil = P(None, "tp")
    return jax.shard_map(
        functools.partial(shards, mesh.shape["ctx"], mesh.shape["tp"]),
        mesh=mesh,
        in_specs=(tok,) * 6 + (P("tp"), fil, fil),
        out_specs=(tok,) * 5 + (fil, fil, P("tp")),
        check_vma=False,
    )
```

```python
import functools
import math

import jax
import jax.numpy as jnp
import ml_dtypes
import numpy as np
from jax import lax
from jax.experimental import pallas as pl
from jax.experimental.pallas import tpu as pltpu
from jax.sharding import PartitionSpec as P

D = 8192
CW = 256
PIECES = 4
F32 = jnp.float32
BF16 = jnp.bfloat16


def split(m):
    hi = m.astype(ml_dtypes.bfloat16)
    lo = (m - hi.astype(np.float64)).astype(ml_dtypes.bfloat16)
    return hi, lo


def matrices(rows):
    n = 2 * rows
    theta = 2.0 * math.pi * (np.arange(rows) + 0.5) / n
    ang = theta[:, None] * np.arange(n)[None, :]
    fwd = np.concatenate([np.cos(ang), -np.sin(ang)], axis=0)
    bwd = np.concatenate([np.cos(ang).T, -np.sin(ang).T], axis=1) / rows
    fh, fl = split(fwd)
    near = np.concatenate([fh[:, :rows], fl[:, :rows]], axis=1)
    bh = bwd.astype(ml_dtypes.bfloat16)
    return np.stack([fh, near, bh])


def body(
    n, ntp, fused,
    vp_h, ks_h, qs_h, km_h, qm_h, og_h, gain_h, fse_h, fmr_h, mats_h,
    o_val, o_qse, o_kse, o_qmr, o_kmr, o_small, o_fmr,
    vp, ks, qs, km, qm, og, gain_in, gain, fse, fmr, mats, in_sem,
    win_se, g2, wsend, wh, conv, fs, gs, gp, win_gs, acc, row_send, row_recv, inv2, k2,
    pfb, own, rc, sx, rx, ag_own, ag_x, ag_c, sm, rs_s, ag_s,
    tail_sem, gh_s, gh_r, wh_s, wh_r, row_s, row_r, gs_sem,
    rc_s, rc_r, rx_s, rx_r, agx_s, agx_r, agc_s, agc_r, rss_s, rss_r, ags_s, ags_r,
):
    me = lax.axis_index("ctx")
    tp = lax.axis_index("tp")
    rows, chans = vp.shape
    taps = fse.shape[0]
    nc = chans // CW
    hc = chans // PIECES
    per = hc // CW
    tiles = CW // 128
    has_l = me > 0
    has_r = me < n - 1
    left = (me + n - 1) % n
    right = (me + 1) % n
    mesh_ids = pl.DeviceIdType.MESH

    def remote(src, dst, ssem, rsem, where):
        return pltpu.make_async_remote_copy(
            src_ref=src, dst_ref=dst, send_sem=ssem, recv_sem=rsem, device_id=where, device_id_type=mesh_ids
        )

    def lanes(c):
        return pl.ds(pl.multiple_of(c * CW, CW), CW)

    def tile(t):
        return pl.ds(pl.multiple_of(t * 128, 128), 128)

    def order(chip, d):
        row, col = chip // 2, chip % 2
        return (row + (4 - d) // 2 * (1 - 2 * row)) * 2 + col + d % 2 * (1 - 2 * col)

    def wide(ref):
        return jnp.concatenate([ref[...]] * (CW // 128), axis=1)

    fetch = [
        pltpu.make_async_copy(src, dst, in_sem.at[i])
        for i, (src, dst) in enumerate(
            [(ks_h, ks), (vp_h, vp), (og_h, og), (qm_h, qm), (mats_h, mats), (fmr_h, fmr), (qs_h, qs), (fse_h, fse),
             (gain_h, gain_in), (km_h, km)]
        )
    ]
    for copy in fetch:
        copy.start()

    bar = pltpu.get_barrier_semaphore()
    ctx_peers = [(me + d) % n for d in range(1, n)] if fused else [left, right]
    for p in ctx_peers:
        pl.semaphore_signal(bar, inc=1, device_id={"ctx": p}, device_id_type=mesh_ids)
    for d in range(1, ntp):
        pl.semaphore_signal(bar, inc=1, device_id={"tp": (tp + d) % ntp}, device_id_type=mesh_ids)

    @pl.when(jnp.logical_not(has_l))
    def _():
        win_se[:, pl.ds(0, 8), :] = jnp.zeros((chans // 128, 8, 128), F32)
        wh[...] = jnp.zeros_like(wh)

    @pl.when(jnp.logical_not(has_r))
    def _():
        g2[pl.ds(rows, rows), :] = jnp.zeros((rows, chans), BF16)
        win_gs[:, pl.ds(rows, 8), :] = jnp.zeros((chans // 128, 8, 128), F32)

    for copy in fetch[:2]:
        copy.wait()

    @pl.loop(0, nc)
    def _(c):
        ch = lanes(c)
        prod = (ks[:, ch].astype(F32) * vp[:, ch].astype(F32)).astype(BF16).astype(F32)
        for i in range(tiles):
            win_se[c * tiles + i, pl.ds(8, rows), :] = prod[:, i * 128 : (i + 1) * 128]

    pl.semaphore_wait(bar, len(ctx_peers) + ntp - 1)

    tail = remote(win_se.at[:, pl.ds(rows, 8)], win_se.at[:, pl.ds(0, 8)], tail_sem.at[0], tail_sem.at[1], {"ctx": right})

    def g_piece(h):
        hl = pl.ds(pl.multiple_of(h * hc, hc), hc)
        return remote(g2.at[pl.ds(0, rows), hl], g2.at[pl.ds(rows, rows), hl], gh_s.at[h], gh_r.at[h], {"ctx": left})

    def w_piece(h):
        hl = pl.ds(pl.multiple_of(h * hc, hc), hc)
        return remote(wsend.at[:, hl], wh.at[:, hl], wh_s.at[h], wh_r.at[h], {"ctx": right})

    @pl.when(has_r)
    def _():
        tail.start()

    for copy in fetch[2:4]:
        copy.wait()

    @pl.loop(0, PIECES)
    def _(h):
        for i in range(per):
            ch = lanes(h * per + i)
            g2[pl.ds(0, rows), ch] = (og[:, ch].astype(F32) * qm[:, ch].astype(F32)).astype(BF16)

        @pl.when(has_l)
        def _():
            g_piece(h).start()

    def twice(x):
        return jnp.concatenate([x, x], axis=0)

    def dot(a, b):
        return jnp.dot(a, b, preferred_element_type=F32)

    def back(re, im, at):
        return dot(mats[2, pl.ds(at, rows), :], jnp.concatenate([re.astype(BF16), im.astype(BF16)], axis=0))

    for copy in fetch[4:6]:
        copy.wait()

    @pl.loop(0, PIECES)
    def _(h):
        for i in range(per):
            ch = lanes(h * per + i)
            fs[:, ch] = dot(mats[1], twice(fmr[:, ch]))

    @pl.when(has_l)
    def _():
        tail.wait_recv()

    for copy in fetch[6:]:
        copy.wait()
    gain[...] = gain_in[...].astype(F32).reshape(1, chans)
    acc[...] = jnp.zeros_like(acc)

    def fold(x):
        s = x[:, :128]
        for i in range(1, CW // 128):
            s = s + x[:, i * 128 : (i + 1) * 128]
        return s

    @pl.loop(0, PIECES)
    def _(h):
        for i in range(hc // 128):
            t = h * (hc // 128) + i
            ch = tile(t)
            f = fse[:, ch].astype(F32)
            cs = win_se[t, pl.ds(8, rows), :] * f[0:1]
            for j in range(1, taps):
                cs = cs + win_se[t, pl.ds(8 - j, rows), :] * f[j : j + 1]
            conv[:, ch] = cs
            mixed = qs[:, ch].astype(F32) * cs
            acc[...] += mixed * mixed

    def share(k):
        row_send[k] = jnp.broadcast_to(jnp.sum(acc[...].T, axis=0, keepdims=True), (8, 128))
        for d in range(1, ntp):
            row_copy(k, d).start()

    def row_copy(k, d):
        return remote(
            row_send.at[k], row_recv.at[k, d - 1], row_s.at[k, d - 1], row_r.at[k, d - 1], {"tp": (tp + d) % ntp}
        )

    def gather(k):
        for d in range(1, ntp):
            row_copy(k, d).wait()
        total = row_send[k]
        for d in range(1, ntp):
            total = total + row_recv[k, d - 1]
        return total

    share(0)

    acc[...] = jnp.zeros_like(acc)

    def input_grad(h):
        @pl.when(has_l)
        def _():
            g_piece(h).wait_send()

        @pl.when(has_r)
        def _():
            g_piece(h).wait_recv()

        for i in range(per):
            ch = lanes(h * per + i)
            g = dot(mats[0], g2[:, ch])
            gs[:, ch] = g
            gr, gi = g[:rows], g[rows:]
            fr, fi = fs[pl.ds(0, rows), ch], fs[pl.ds(rows, rows), ch]
            grad = back(gr * fr + gi * fi, gi * fr - gr * fi, 0)
            gp[:, ch] = grad
            mixed = qs[:, ch].astype(F32) * conv[:, ch]
            acc[...] += fold(grad * km[:, ch].astype(F32) * gain[:, ch] * mixed)

    pl.loop(0, PIECES)(input_grad)
    share(1)

    inv_row = lax.rsqrt(gather(0) / D + 1e-06)
    inv2[...] = jnp.broadcast_to(inv_row[0:1], (128, 128)).T

    def medium(c):
        ch = lanes(c)
        mixed = qs[:, ch].astype(F32) * conv[:, ch]
        normed = (mixed * wide(inv2) * gain[:, ch]).astype(BF16).astype(F32)
        prod = (km[:, ch].astype(F32) * normed).astype(BF16)
        wsend[:, ch] = prod
        o_kmr[:, ch] = (gp[:, ch] * normed).astype(BF16)
        x = dot(mats[1], twice(prod))
        xr, xi = x[:rows], x[rows:]
        gr, gi = gs[pl.ds(0, rows), ch], gs[pl.ds(rows, rows), ch]
        return back(gr * xr + gi * xi, gi * xr - gr * xi, 0)

    def medium_out(c):
        ch = lanes(c)
        x = dot(mats[0], jnp.concatenate([wh[:, ch], wsend[:, ch]], axis=0))
        xr, xi = x[:rows], x[rows:]
        fr, fi = fs[pl.ds(0, rows), ch], fs[pl.ds(rows, rows), ch]
        y = back(xr * fr - xi * fi, xr * fi + xi * fr, rows)
        o_qmr[:, ch] = (og[:, ch].astype(F32) * y).astype(BF16)

    if fused:
        chips = n // 2
        core = me % 2
        chip = me // 2
        mate = me + 1 - 2 * core

        def to_mate(i):
            return remote(pfb.at[i], rc.at[i], rc_s.at[i], rc_r.at[i], {"ctx": mate})

        cy, cx = chip // 2, chip % 2
        over_y = ((1 - cy) * 2 + cx) * 2 + core
        over_x = (cy * 2 + 1 - cx) * 2 + core

        def to_y(k):
            return remote(sx.at[k], rx.at[k], rx_s.at[k], rx_r.at[k], {"ctx": over_y})

        def to_x():
            return remote(sx.at[2], rx.at[2], rx_s.at[2], rx_r.at[2], {"ctx": over_x})

        def all_x():
            return remote(ag_own, ag_x.at[0], agx_s.at[0], agx_r.at[0], {"ctx": over_x})

        def all_y(k):
            src = ag_own if k == 0 else ag_x.at[0]
            return remote(src, ag_x.at[1 + k], agx_s.at[1 + k], agx_r.at[1 + k], {"ctx": over_y})

        def all_mate(d):
            src = ag_own if d == 0 else ag_x.at[d - 1]
            return remote(src, ag_c.at[d], agc_s.at[d], agc_r.at[d], {"ctx": mate})

        @pl.loop(1, chips + 1)
        def _(d):
            c = order(chip, d)
            theirs = medium(2 * c + 1 - core)
            ours = medium(2 * c + core)
            pfb[c] = theirs.astype(BF16)
            to_mate(c).start()
            own[c] = ours

            @pl.when(has_r)
            def _():
                w_piece(c).start()

            @pl.when((d > 1) & (d < chips))
            def _():
                before = order(chip, d - 1)
                to_mate(before).wait_recv()
                sx[d - 2] = (own[before] + rc[before].astype(F32)).astype(BF16)
                to_y(d - 2).start()

        before = order(chip, 3)
        to_mate(before).wait_recv()
        to_y(0).wait_recv()
        sx[2] = (own[before] + rc[before].astype(F32) + rx[0].astype(F32)).astype(BF16)
        to_x().start()
    else:

        @pl.loop(0, PIECES)
        def _(h):
            for i in range(per):
                c = h * per + i
                o_fmr[:, lanes(c)] = medium(c).astype(o_fmr.dtype)

            @pl.when(has_r)
            def _():
                w_piece(h).start()

    dot_row = gather(1)
    inv = inv2[...]
    k2[...] = inv * inv * inv * jnp.broadcast_to(dot_row[0:1], (128, 128)).T / D

    @pl.loop(0, nc)
    def _(c):
        for i in range(tiles):
            t = c * tiles + i
            at = pl.ds(i * 128, 128)
            ch = tile(t)
            cs = conv[:, ch]
            q = qs[:, ch].astype(F32)
            mixed = q * cs
            grad_normed = gp[:, ch] * km[:, ch].astype(F32)
            grad_mixed = inv2[...] * (grad_normed * gain[:, ch]) - mixed * k2[...]
            o_qse[:, ch] = (grad_mixed * cs).astype(BF16)
            sm[c, pl.ds(taps, 1), at] = jnp.sum(grad_normed * mixed * inv2[...], axis=0, keepdims=True)
            gcs = (grad_mixed * q).astype(BF16).astype(F32)
            win_gs[t, pl.ds(0, rows), :] = gcs
            for j in range(taps):
                sm[c, pl.ds(j, 1), at] = jnp.sum(gcs * win_se[t, pl.ds(8 - j, rows), :], axis=0, keepdims=True)

    head = remote(win_gs.at[:, pl.ds(0, 8)], win_gs.at[:, pl.ds(rows, 8)], gs_sem.at[0], gs_sem.at[1], {"ctx": left})

    @pl.when(has_l)
    def _():
        head.start()

    if fused:

        def small_to(d):
            return remote(
                sm.at[(me + d) % n], rs_s.at[d - 1], rss_s.at[d - 1], rss_r.at[d - 1], {"ctx": (me + d) % n}
            )

        def small_all(d):
            return remote(
                ag_s.at[0], ag_s.at[d], ags_s.at[d - 1], ags_r.at[d - 1], {"ctx": (me + d) % n}
            )

        for d in range(1, n):
            small_to(d).start()

        to_mate(chip).wait_recv()
        total = own[chip] + rc[chip].astype(F32)
        to_y(1).wait_recv()
        to_x().wait_recv()
        total = total + rx[1].astype(F32) + rx[2].astype(F32)
        ag_own[...] = total.astype(BF16)
        all_x().start()
        all_y(0).start()
        all_mate(0).start()

    def medium_piece(step):
        h = order((left // 2) % PIECES, step + 1)

        @pl.when(has_l)
        def _():
            w_piece(h).wait_recv()

        for i in range(per):
            medium_out(h * per + i)

    pl.loop(0, PIECES // 2)(medium_piece)

    if fused:
        all_x().wait_recv()
        all_y(1).start()
        all_mate(1).start()
        total_s = sm[me]
        for d in range(1, n):
            small_to(d).wait_recv()
            total_s = total_s + rs_s[d - 1]
        ag_s[0] = total_s
        for d in range(1, n):
            small_all(d).start()

    pl.loop(PIECES // 2, PIECES)(medium_piece)

    if fused:
        for k in range(2):
            all_y(k).wait_recv()
            all_mate(2 + k).start()

    @pl.when(has_r)
    def _():
        head.wait_recv()

    @pl.loop(0, nc)
    def _(c):
        for i in range(tiles):
            t = c * tiles + i
            ch = tile(t)
            f = fse[:, ch].astype(F32)
            g = win_gs[t, pl.ds(0, rows), :] * f[0:1]
            for j in range(1, taps):
                g = g + win_gs[t, pl.ds(j, rows), :] * f[j : j + 1]
            o_kse[:, ch] = (g * vp[:, ch].astype(F32)).astype(BF16)
            o_val[:, ch] = (g * ks[:, ch].astype(F32)).astype(BF16)

    if fused:
        o_fmr[:, lanes(me)] = ag_own[...]
        blocks = (chip, order(chip, 3), order(chip, 2), order(chip, 1))
        for k in range(1, chips):
            o_fmr[:, lanes(blocks[k] * 2 + core)] = ag_x[k - 1]
        o_small[:, lanes(me)] = ag_s[0]
        for d in range(1, n):
            small_all(d).wait_recv()
            o_small[:, lanes((me + n - d) % n)] = ag_s[d]
        for d in range(chips):
            all_mate(d).wait_recv()
            o_fmr[:, lanes(blocks[d] * 2 + 1 - core)] = ag_c[d]
        for i in range(chips):
            to_mate(i).wait_send()
            all_mate(i).wait_send()
        for k in range(2):
            to_y(k).wait_send()
            all_y(k).wait_send()
        to_x().wait_send()
        all_x().wait_send()
        for d in range(1, n):
            small_to(d).wait_send()
            small_all(d).wait_send()
    else:

        @pl.loop(0, nc)
        def _(c):
            o_small[:, lanes(c)] = sm[c]

    @pl.when(has_l)
    def _():
        head.wait_send()

    @pl.when(has_r)
    def _():
        tail.wait_send()
        for h in range(PIECES):
            w_piece(h).wait_send()


def write_out(val, qse, kse, qmr, kmr, small, gf, *rest):
    outs, (o_fse, o_fmr, o_gain, fse, fmr, gain, sem) = rest[:5], rest[5:]
    copies = [pltpu.make_async_copy(a, b, sem.at[i]) for i, (a, b) in enumerate(zip((val, qse, kse, qmr, kmr), outs))]
    for copy in copies:
        copy.start()
    taps = fse.shape[0]
    part = fmr.shape[0] // 4
    for i in range(4):
        at = pl.ds(i * part, part)
        fmr[at, :] = gf[at, :].astype(F32)
        copies.append(pltpu.make_async_copy(fmr.at[at], o_fmr.at[at], sem.at[5 + i]))
        copies[-1].start()
    fse[...] = small[pl.ds(0, taps), :]
    gain[...] = small[pl.ds(taps, 1), :]
    copies.append(pltpu.make_async_copy(fse, o_fse, sem.at[9]))
    copies.append(pltpu.make_async_copy(gain, o_gain, sem.at[10]))
    copies[-2].start()
    copies[-1].start()
    for copy in copies:
        copy.wait()


def shards(n, ntp, vp, ks, qs, km, qm, og, norm_gain, fse, fmr):
    rows, chans = vp.shape
    taps = fse.shape[0]
    nc = chans // CW
    fused = n == nc and n == 2 * PIECES
    chips = max(n // 2, 2) if fused else 2
    blk = (rows, CW)
    peers = n if fused else 2
    wide_out = jax.ShapeDtypeStruct((rows, chans), BF16)
    dma = pltpu.SemaphoreType.DMA
    vmem = pltpu.VMEM
    scratch = [vmem((rows, chans), BF16) for _ in range(6)] + [
        vmem((chans,), BF16),
        vmem((1, chans), F32),
        vmem((taps, chans), BF16),
        vmem(fmr.shape, BF16),
        vmem((3, 2 * rows, 2 * rows), BF16),
        dma((10,)),
        vmem((chans // 128, rows + 8, 128), F32),
        vmem((2 * rows, chans), BF16),
        vmem((rows, chans), BF16),
        vmem((rows, chans), BF16),
        vmem((rows, chans), F32),
        vmem((2 * rows, chans), F32),
        vmem((2 * rows, chans), F32),
        vmem((rows, chans), F32),
        vmem((chans // 128, rows + 8, 128), F32),
        vmem((rows, 128), F32),
        vmem((2, 8, 128), F32),
        vmem((2, ntp - 1, 8, 128), F32),
        vmem((rows, 128), F32),
        vmem((rows, 128), F32),
        vmem((chips,) + blk, BF16),
        vmem((chips,) + blk, F32),
        vmem((chips,) + blk, BF16),
        vmem((chips - 1,) + blk, BF16),
        vmem((chips - 1,) + blk, BF16),
        vmem(blk, BF16),
        vmem((chips - 1,) + blk, BF16),
        vmem((chips,) + blk, BF16),
        vmem((nc, taps + 1, CW), F32),
        vmem((peers - 1, taps + 1, CW), F32),
        vmem((peers, taps + 1, CW), F32),
        dma((2,)),
        dma((PIECES,)), dma((PIECES,)),
        dma((PIECES,)), dma((PIECES,)),
        dma((2, ntp - 1)), dma((2, ntp - 1)),
        dma((2,)),
        dma((chips,)), dma((chips,)),
        dma((chips - 1,)), dma((chips - 1,)),
        dma((chips - 1,)), dma((chips - 1,)),
        dma((chips,)), dma((chips,)),
        dma((peers - 1,)), dma((peers - 1,)),
        dma((peers - 1,)), dma((peers - 1,)),
    ]
    spec = pl.BlockSpec(memory_space=pltpu.VMEM)
    mats = jnp.asarray(matrices(rows))
    operands = (vp, ks, qs, km, qm, og, norm_gain, fse, fmr, mats)
    outs = pl.pallas_call(
        functools.partial(body, n, ntp, fused),
        out_shape=[wide_out] * 5
        + [jax.ShapeDtypeStruct((taps + 1, chans), F32), jax.ShapeDtypeStruct((rows, chans), BF16 if fused else F32)],
        in_specs=[pl.BlockSpec(memory_space=pltpu.HBM)] * 10,
        out_specs=[spec] * 7,
        scratch_shapes=scratch,
        compiler_params=pltpu.CompilerParams(
            collective_id=0, has_side_effects=True, vmem_limit_bytes=40 * 1024 * 1024
        ),
        name="hyena_backward",
    )(*(pltpu.with_memory_space_constraint(x, pltpu.HBM) for x in operands))
    if not fused:
        small, gf = lax.psum(outs[5:], "ctx")
        outs = list(outs[:5]) + [small, gf]
    hbm = pl.BlockSpec(memory_space=pltpu.HBM)
    done = pl.pallas_call(
        write_out,
        out_shape=[wide_out] * 5
        + [
            jax.ShapeDtypeStruct((taps, chans), F32),
            jax.ShapeDtypeStruct((rows, chans), F32),
            jax.ShapeDtypeStruct((1, chans), F32),
        ],
        in_specs=[spec] * 7,
        out_specs=[hbm] * 8,
        scratch_shapes=[vmem((taps, chans), F32), vmem((rows, chans), F32), vmem((1, chans), F32), dma((11,))],
        compiler_params=pltpu.CompilerParams(vmem_limit_bytes=12 * 1024 * 1024),
        name="write_out",
    )(*outs)
    return tuple(done[:7]) + (done[7].reshape(chans),)


def solution(mesh):
    tok = P("ctx", "tp")
    fil = P(None, "tp")
    return jax.shard_map(
        functools.partial(shards, mesh.shape["ctx"], mesh.shape["tp"]),
        mesh=mesh,
        in_specs=(tok,) * 6 + (P("tp"), fil, fil),
        out_specs=(tok,) * 5 + (fil, fil, P("tp")),
        check_vma=False,
    )
```

```python
import functools
import math

import jax
import jax.numpy as jnp
import ml_dtypes
import numpy as np
from jax import lax
from jax.experimental import pallas as pl
from jax.experimental.pallas import tpu as pltpu
from jax.sharding import PartitionSpec as P

D = 8192
CW = 256
PIECES = 4
F32 = jnp.float32
BF16 = jnp.bfloat16


def split(m):
    hi = m.astype(ml_dtypes.bfloat16)
    lo = (m - hi.astype(np.float64)).astype(ml_dtypes.bfloat16)
    return hi, lo


def matrices(rows):
    n = 2 * rows
    theta = 2.0 * math.pi * (np.arange(rows) + 0.5) / n
    ang = theta[:, None] * np.arange(n)[None, :]
    fwd = np.concatenate([np.cos(ang), -np.sin(ang)], axis=0)
    bwd = np.concatenate([np.cos(ang).T, -np.sin(ang).T], axis=1) / rows
    fh, fl = split(fwd)
    near = np.concatenate([fh[:, :rows], fl[:, :rows]], axis=1)
    bh = bwd.astype(ml_dtypes.bfloat16)
    return np.stack([fh, near, bh])


def body(
    n, ntp, fused,
    vp_h, ks_h, qs_h, km_h, qm_h, og_h, gain_h, fse_h, fmr_h, mats_h,
    o_val, o_qse, o_kse, o_qmr, o_kmr, o_small, o_fmr,
    vp, ks, qs, km, qm, og, gain_in, gain, fse, fmr, mats, in_sem,
    win_se, g2, wsend, wh, pr, conv, fs, gs, gp, win_gs, acc, row_send, row_recv, inv_send, invl_row, inv2, invl2, k2,
    pfb, own, rc, sx, rx, ag_own, ag_x, ag_c, sm, rs_s, ag_s,
    tail_sem, gh_s, gh_r, wh_s, wh_r, row_s, row_r, inv_sem, gs_sem,
    rc_s, rc_r, rx_s, rx_r, agx_s, agx_r, agc_s, agc_r, rss_s, rss_r, ags_s, ags_r,
):
    me = lax.axis_index("ctx")
    tp = lax.axis_index("tp")
    rows, chans = vp.shape
    taps = fse.shape[0]
    nc = chans // CW
    hc = chans // PIECES
    per = hc // CW
    tiles = CW // 128
    has_l = me > 0
    has_r = me < n - 1
    left = (me + n - 1) % n
    right = (me + 1) % n
    mesh_ids = pl.DeviceIdType.MESH

    def remote(src, dst, ssem, rsem, where):
        return pltpu.make_async_remote_copy(
            src_ref=src, dst_ref=dst, send_sem=ssem, recv_sem=rsem, device_id=where, device_id_type=mesh_ids
        )

    def lanes(c):
        return pl.ds(pl.multiple_of(c * CW, CW), CW)

    def tile(t):
        return pl.ds(pl.multiple_of(t * 128, 128), 128)

    def wide(ref):
        return jnp.concatenate([ref[...]] * (CW // 128), axis=1)

    fetch = [
        pltpu.make_async_copy(src, dst, in_sem.at[i])
        for i, (src, dst) in enumerate(
            [(ks_h, ks), (vp_h, vp), (og_h, og), (qm_h, qm), (mats_h, mats), (fmr_h, fmr), (qs_h, qs), (fse_h, fse),
             (gain_h, gain_in), (km_h, km)]
        )
    ]
    for copy in fetch:
        copy.start()

    bar = pltpu.get_barrier_semaphore()
    ctx_peers = [(me + d) % n for d in range(1, n)] if fused else [left, right]
    for p in ctx_peers:
        pl.semaphore_signal(bar, inc=1, device_id={"ctx": p}, device_id_type=mesh_ids)
    for d in range(1, ntp):
        pl.semaphore_signal(bar, inc=1, device_id={"tp": (tp + d) % ntp}, device_id_type=mesh_ids)

    @pl.when(jnp.logical_not(has_l))
    def _():
        win_se[:, pl.ds(0, 8), :] = jnp.zeros((chans // 128, 8, 128), F32)
        wh[...] = jnp.zeros_like(wh)
        invl_row[...] = jnp.zeros_like(invl_row)

    @pl.when(jnp.logical_not(has_r))
    def _():
        g2[pl.ds(rows, rows), :] = jnp.zeros((rows, chans), BF16)
        win_gs[:, pl.ds(rows, 8), :] = jnp.zeros((chans // 128, 8, 128), F32)

    for copy in fetch[:2]:
        copy.wait()

    @pl.loop(0, nc)
    def _(c):
        ch = lanes(c)
        prod = (ks[:, ch].astype(F32) * vp[:, ch].astype(F32)).astype(BF16).astype(F32)
        for i in range(tiles):
            win_se[c * tiles + i, pl.ds(8, rows), :] = prod[:, i * 128 : (i + 1) * 128]

    pl.semaphore_wait(bar, len(ctx_peers) + ntp - 1)

    tail = remote(win_se.at[:, pl.ds(rows, 8)], win_se.at[:, pl.ds(0, 8)], tail_sem.at[0], tail_sem.at[1], {"ctx": right})

    def g_piece(h):
        hl = pl.ds(pl.multiple_of(h * hc, hc), hc)
        return remote(g2.at[pl.ds(0, rows), hl], g2.at[pl.ds(rows, rows), hl], gh_s.at[h], gh_r.at[h], {"ctx": left})

    def w_piece(h):
        hl = pl.ds(pl.multiple_of(h * hc, hc), hc)
        return remote(wsend.at[:, hl], wh.at[:, hl], wh_s.at[h], wh_r.at[h], {"ctx": right})

    @pl.when(has_r)
    def _():
        tail.start()

    for copy in fetch[2:4]:
        copy.wait()

    @pl.loop(0, PIECES)
    def _(h):
        for i in range(per):
            ch = lanes(h * per + i)
            g2[pl.ds(0, rows), ch] = (og[:, ch].astype(F32) * qm[:, ch].astype(F32)).astype(BF16)

        @pl.when(has_l)
        def _():
            g_piece(h).start()

    def twice(x):
        return jnp.concatenate([x, x], axis=0)

    def dot(a, b):
        return jnp.dot(a, b, preferred_element_type=F32)

    def back(re, im, at):
        return dot(mats[2, pl.ds(at, rows), :], jnp.concatenate([re.astype(BF16), im.astype(BF16)], axis=0))

    for copy in fetch[4:6]:
        copy.wait()

    @pl.loop(0, PIECES)
    def _(h):
        for i in range(per):
            ch = lanes(h * per + i)
            fs[:, ch] = dot(mats[1], twice(fmr[:, ch]))

    @pl.when(has_l)
    def _():
        tail.wait_recv()

    for copy in fetch[6:]:
        copy.wait()
    gain[...] = gain_in[...].astype(F32).reshape(1, chans)
    acc[...] = jnp.zeros_like(acc)

    def fold(x):
        s = x[:, :128]
        for i in range(1, CW // 128):
            s = s + x[:, i * 128 : (i + 1) * 128]
        return s

    @pl.loop(0, PIECES)
    def _(h):
        for i in range(hc // 128):
            t = h * (hc // 128) + i
            ch = tile(t)
            f = fse[:, ch].astype(F32)
            cs = win_se[t, pl.ds(8, rows), :] * f[0:1]
            for j in range(1, taps):
                cs = cs + win_se[t, pl.ds(8 - j, rows), :] * f[j : j + 1]
            conv[:, ch] = cs
            mixed = qs[:, ch].astype(F32) * cs
            acc[...] += mixed * mixed
            wsend[:, ch] = (mixed * gain[:, ch] * km[:, ch].astype(F32)).astype(BF16)

        @pl.when(has_r)
        def _():
            w_piece(h).start()

    def share(k):
        row_send[k] = jnp.broadcast_to(jnp.sum(acc[...].T, axis=0, keepdims=True), (8, 128))
        for d in range(1, ntp):
            row_copy(k, d).start()

    def row_copy(k, d):
        return remote(
            row_send.at[k], row_recv.at[k, d - 1], row_s.at[k, d - 1], row_r.at[k, d - 1], {"tp": (tp + d) % ntp}
        )

    def gather(k):
        for d in range(1, ntp):
            row_copy(k, d).wait()
        total = row_send[k]
        for d in range(1, ntp):
            total = total + row_recv[k, d - 1]
        return total

    share(0)

    acc[...] = jnp.zeros_like(acc)

    def input_grad(h):
        @pl.when(has_l)
        def _():
            g_piece(h).wait_send()

        @pl.when(has_r)
        def _():
            g_piece(h).wait_recv()

        for i in range(per):
            ch = lanes(h * per + i)
            g = dot(mats[0], g2[:, ch])
            gs[:, ch] = g
            gr, gi = g[:rows], g[rows:]
            fr, fi = fs[pl.ds(0, rows), ch], fs[pl.ds(rows, rows), ch]
            grad = back(gr * fr + gi * fi, gi * fr - gr * fi, 0)
            gp[:, ch] = grad
            mixed = qs[:, ch].astype(F32) * conv[:, ch]
            acc[...] += fold(grad * km[:, ch].astype(F32) * gain[:, ch] * mixed)

    pl.loop(0, PIECES)(input_grad)
    share(1)

    inv_row = lax.rsqrt(gather(0) / D + 1e-06)
    inv_send[...] = inv_row
    inv_copy = remote(inv_send, invl_row, inv_sem.at[0], inv_sem.at[1], {"ctx": right})

    @pl.when(has_r)
    def _():
        inv_copy.start()

    inv2[...] = jnp.broadcast_to(inv_row[0:1], (128, 128)).T

    def medium(c):
        ch = lanes(c)
        mixed = qs[:, ch].astype(F32) * conv[:, ch]
        normed = (mixed * wide(inv2) * gain[:, ch]).astype(BF16).astype(F32)
        prod = (km[:, ch].astype(F32) * normed).astype(BF16)
        pr[:, ch] = prod
        o_kmr[:, ch] = (gp[:, ch] * normed).astype(BF16)
        x = dot(mats[1], twice(prod))
        xr, xi = x[:rows], x[rows:]
        gr, gi = gs[pl.ds(0, rows), ch], gs[pl.ds(rows, rows), ch]
        return back(gr * xr + gi * xi, gi * xr - gr * xi, 0)

    def medium_out(c):
        ch = lanes(c)
        halo = (wh[:, ch].astype(F32) * wide(invl2)).astype(BF16)
        x = dot(mats[0], jnp.concatenate([halo, pr[:, ch]], axis=0))
        xr, xi = x[:rows], x[rows:]
        fr, fi = fs[pl.ds(0, rows), ch], fs[pl.ds(rows, rows), ch]
        y = back(xr * fr - xi * fi, xr * fi + xi * fr, rows)
        o_qmr[:, ch] = (og[:, ch].astype(F32) * y).astype(BF16)

    if fused:
        chips = n // 2
        core = me % 2
        chip = me // 2
        mate = me + 1 - 2 * core

        def to_mate(i):
            return remote(pfb.at[i], rc.at[i], rc_s.at[i], rc_r.at[i], {"ctx": mate})

        def to_chip(d):
            return remote(
                sx.at[d - 1], rx.at[d - 1], rx_s.at[d - 1], rx_r.at[d - 1], {"ctx": ((chip + d) % chips) * 2 + core}
            )

        def all_chip(d):
            return remote(
                ag_own, ag_x.at[d - 1], agx_s.at[d - 1], agx_r.at[d - 1], {"ctx": ((chip + d) % chips) * 2 + core}
            )

        def all_mate(d):
            src = ag_own if d == 0 else ag_x.at[d - 1]
            return remote(src, ag_c.at[d], agc_s.at[d], agc_r.at[d], {"ctx": mate})

        @pl.loop(1, chips + 1)
        def _(d):
            c = (chip + d) % chips

            theirs = medium(2 * c + 1 - core)
            ours = medium(2 * c + core)
            pfb[c] = theirs.astype(BF16)
            to_mate(c).start()
            own[c] = ours

            @pl.when(d > 1)
            def _():
                before = (chip + d - 1) % chips
                to_mate(before).wait_recv()
                sx[d - 2] = (own[before] + rc[before].astype(F32)).astype(BF16)
                to_chip(d - 1).start()
    else:

        @pl.loop(0, PIECES)
        def _(h):
            for i in range(per):
                c = h * per + i
                o_fmr[:, lanes(c)] = medium(c).astype(o_fmr.dtype)

    dot_row = gather(1)
    inv = inv2[...]
    k2[...] = inv * inv * inv * jnp.broadcast_to(dot_row[0:1], (128, 128)).T / D

    @pl.loop(0, nc)
    def _(c):
        for i in range(tiles):
            t = c * tiles + i
            at = pl.ds(i * 128, 128)
            ch = tile(t)
            cs = conv[:, ch]
            q = qs[:, ch].astype(F32)
            mixed = q * cs
            grad_normed = gp[:, ch] * km[:, ch].astype(F32)
            grad_mixed = inv2[...] * (grad_normed * gain[:, ch]) - mixed * k2[...]
            o_qse[:, ch] = (grad_mixed * cs).astype(BF16)
            sm[c, pl.ds(taps, 1), at] = jnp.sum(grad_normed * mixed * inv2[...], axis=0, keepdims=True)
            gcs = (grad_mixed * q).astype(BF16).astype(F32)
            win_gs[t, pl.ds(0, rows), :] = gcs
            for j in range(taps):
                sm[c, pl.ds(j, 1), at] = jnp.sum(gcs * win_se[t, pl.ds(8 - j, rows), :], axis=0, keepdims=True)

    head = remote(win_gs.at[:, pl.ds(0, 8)], win_gs.at[:, pl.ds(rows, 8)], gs_sem.at[0], gs_sem.at[1], {"ctx": left})

    @pl.when(has_l)
    def _():
        head.start()

    if fused:

        def small_to(d):
            return remote(
                sm.at[(me + d) % n], rs_s.at[d - 1], rss_s.at[d - 1], rss_r.at[d - 1], {"ctx": (me + d) % n}
            )

        def small_all(d):
            return remote(
                ag_s.at[0], ag_s.at[d], ags_s.at[d - 1], ags_r.at[d - 1], {"ctx": (me + d) % n}
            )

        for d in range(1, n):
            small_to(d).start()

        to_mate(chip).wait_recv()
        total = own[chip] + rc[chip].astype(F32)
        for d in range(1, chips):
            to_chip(d).wait_recv()
            total = total + rx[d - 1].astype(F32)
        ag_own[...] = total.astype(BF16)
        for d in range(1, chips):
            all_chip(d).start()
        all_mate(0).start()

    @pl.when(has_l)
    def _():
        inv_copy.wait_recv()

    invl2[...] = jnp.broadcast_to(invl_row[0:1], (128, 128)).T

    def medium_piece(h):
        @pl.when(has_l)
        def _():
            w_piece(h).wait_recv()

        for i in range(per):
            medium_out(h * per + i)

    pl.loop(0, PIECES // 2)(medium_piece)

    if fused:
        total_s = sm[me]
        for d in range(1, n):
            small_to(d).wait_recv()
            total_s = total_s + rs_s[d - 1]
        ag_s[0] = total_s
        for d in range(1, n):
            small_all(d).start()

    pl.loop(PIECES // 2, PIECES)(medium_piece)

    if fused:
        for d in range(1, chips):
            all_chip(d).wait_recv()
            all_mate(d).start()

    @pl.when(has_r)
    def _():
        head.wait_recv()

    @pl.loop(0, nc)
    def _(c):
        for i in range(tiles):
            t = c * tiles + i
            ch = tile(t)
            f = fse[:, ch].astype(F32)
            g = win_gs[t, pl.ds(0, rows), :] * f[0:1]
            for j in range(1, taps):
                g = g + win_gs[t, pl.ds(j, rows), :] * f[j : j + 1]
            o_kse[:, ch] = (g * vp[:, ch].astype(F32)).astype(BF16)
            o_val[:, ch] = (g * ks[:, ch].astype(F32)).astype(BF16)

    if fused:
        o_fmr[:, lanes(me)] = ag_own[...]
        for d in range(1, chips):
            o_fmr[:, lanes(((chip + chips - d) % chips) * 2 + core)] = ag_x[d - 1]
        o_small[:, lanes(me)] = ag_s[0]
        for d in range(1, n):
            small_all(d).wait_recv()
            o_small[:, lanes((me + n - d) % n)] = ag_s[d]
        for d in range(chips):
            all_mate(d).wait_recv()
            o_fmr[:, lanes(((chip + chips - d) % chips) * 2 + 1 - core)] = ag_c[d]
        for i in range(chips):
            to_mate(i).wait_send()
            all_mate(i).wait_send()
        for d in range(1, chips):
            to_chip(d).wait_send()
            all_chip(d).wait_send()
        for d in range(1, n):
            small_to(d).wait_send()
            small_all(d).wait_send()
    else:

        @pl.loop(0, nc)
        def _(c):
            o_small[:, lanes(c)] = sm[c]

    @pl.when(has_l)
    def _():
        head.wait_send()

    @pl.when(has_r)
    def _():
        tail.wait_send()
        inv_copy.wait_send()
        for h in range(PIECES):
            w_piece(h).wait_send()


def write_out(val, qse, kse, qmr, kmr, small, gf, *rest):
    outs, (o_fse, o_fmr, o_gain, fse, fmr, gain, sem) = rest[:5], rest[5:]
    copies = [pltpu.make_async_copy(a, b, sem.at[i]) for i, (a, b) in enumerate(zip((val, qse, kse, qmr, kmr), outs))]
    for copy in copies:
        copy.start()
    taps = fse.shape[0]
    part = fmr.shape[0] // 4
    for i in range(4):
        at = pl.ds(i * part, part)
        fmr[at, :] = gf[at, :].astype(F32)
        copies.append(pltpu.make_async_copy(fmr.at[at], o_fmr.at[at], sem.at[5 + i]))
        copies[-1].start()
    fse[...] = small[pl.ds(0, taps), :]
    gain[...] = small[pl.ds(taps, 1), :]
    copies.append(pltpu.make_async_copy(fse, o_fse, sem.at[9]))
    copies.append(pltpu.make_async_copy(gain, o_gain, sem.at[10]))
    copies[-2].start()
    copies[-1].start()
    for copy in copies:
        copy.wait()


def shards(n, ntp, vp, ks, qs, km, qm, og, norm_gain, fse, fmr):
    rows, chans = vp.shape
    taps = fse.shape[0]
    nc = chans // CW
    fused = n == nc and n % 2 == 0
    chips = max(n // 2, 2) if fused else 2
    blk = (rows, CW)
    peers = n if fused else 2
    wide_out = jax.ShapeDtypeStruct((rows, chans), BF16)
    dma = pltpu.SemaphoreType.DMA
    vmem = pltpu.VMEM
    scratch = [vmem((rows, chans), BF16) for _ in range(6)] + [
        vmem((chans,), BF16),
        vmem((1, chans), F32),
        vmem((taps, chans), BF16),
        vmem(fmr.shape, BF16),
        vmem((3, 2 * rows, 2 * rows), BF16),
        dma((10,)),
        vmem((chans // 128, rows + 8, 128), F32),
        vmem((2 * rows, chans), BF16),
        vmem((rows, chans), BF16),
        vmem((rows, chans), BF16),
        vmem((rows, chans), BF16),
        vmem((rows, chans), F32),
        vmem((2 * rows, chans), F32),
        vmem((2 * rows, chans), F32),
        vmem((rows, chans), F32),
        vmem((chans // 128, rows + 8, 128), F32),
        vmem((rows, 128), F32),
        vmem((2, 8, 128), F32),
        vmem((2, ntp - 1, 8, 128), F32),
        vmem((8, 128), F32),
        vmem((8, 128), F32),
        vmem((rows, 128), F32),
        vmem((rows, 128), F32),
        vmem((rows, 128), F32),
        vmem((chips,) + blk, BF16),
        vmem((chips,) + blk, F32),
        vmem((chips,) + blk, BF16),
        vmem((chips - 1,) + blk, BF16),
        vmem((chips - 1,) + blk, BF16),
        vmem(blk, BF16),
        vmem((chips - 1,) + blk, BF16),
        vmem((chips,) + blk, BF16),
        vmem((nc, taps + 1, CW), F32),
        vmem((peers - 1, taps + 1, CW), F32),
        vmem((peers, taps + 1, CW), F32),
        dma((2,)),
        dma((PIECES,)), dma((PIECES,)),
        dma((PIECES,)), dma((PIECES,)),
        dma((2, ntp - 1)), dma((2, ntp - 1)),
        dma((2,)),
        dma((2,)),
        dma((chips,)), dma((chips,)),
        dma((chips - 1,)), dma((chips - 1,)),
        dma((chips - 1,)), dma((chips - 1,)),
        dma((chips,)), dma((chips,)),
        dma((peers - 1,)), dma((peers - 1,)),
        dma((peers - 1,)), dma((peers - 1,)),
    ]
    spec = pl.BlockSpec(memory_space=pltpu.VMEM)
    mats = jnp.asarray(matrices(rows))
    operands = (vp, ks, qs, km, qm, og, norm_gain, fse, fmr, mats)
    outs = pl.pallas_call(
        functools.partial(body, n, ntp, fused),
        out_shape=[wide_out] * 5
        + [jax.ShapeDtypeStruct((taps + 1, chans), F32), jax.ShapeDtypeStruct((rows, chans), BF16 if fused else F32)],
        in_specs=[pl.BlockSpec(memory_space=pltpu.HBM)] * 10,
        out_specs=[spec] * 7,
        scratch_shapes=scratch,
        compiler_params=pltpu.CompilerParams(
            collective_id=0, has_side_effects=True, vmem_limit_bytes=40 * 1024 * 1024
        ),
        name="hyena_backward",
    )(*(pltpu.with_memory_space_constraint(x, pltpu.HBM) for x in operands))
    if not fused:
        small, gf = lax.psum(outs[5:], "ctx")
        outs = list(outs[:5]) + [small, gf]
    hbm = pl.BlockSpec(memory_space=pltpu.HBM)
    done = pl.pallas_call(
        write_out,
        out_shape=[wide_out] * 5
        + [
            jax.ShapeDtypeStruct((taps, chans), F32),
            jax.ShapeDtypeStruct((rows, chans), F32),
            jax.ShapeDtypeStruct((1, chans), F32),
        ],
        in_specs=[spec] * 7,
        out_specs=[hbm] * 8,
        scratch_shapes=[vmem((taps, chans), F32), vmem((rows, chans), F32), vmem((1, chans), F32), dma((11,))],
        compiler_params=pltpu.CompilerParams(vmem_limit_bytes=12 * 1024 * 1024),
        name="write_out",
    )(*outs)
    return tuple(done[:7]) + (done[7].reshape(chans),)


def solution(mesh):
    tok = P("ctx", "tp")
    fil = P(None, "tp")
    return jax.shard_map(
        functools.partial(shards, mesh.shape["ctx"], mesh.shape["tp"]),
        mesh=mesh,
        in_specs=(tok,) * 6 + (P("tp"), fil, fil),
        out_specs=(tok,) * 5 + (fil, fil, P("tp")),
        check_vma=False,
    )
```
